32 devices in a mesh: lon: 8 (over y, x, core), lat: 4 (over z).
Axes of the slice: x: 2, y: 2, z: 4, core: 2. Of those that a mesh axis runs over, the one named last changes fastest.
Arguments:
- winds: bfloat16 [2, 32, 4, 384, 512], P(None, None, None, 'lon', 'lat'), may hold values from -60 to 60
Outputs:
- basis: float32 [48, 2, 4, 384, 512], P(None, None, None, 'lon', 'lat')
The draws below stay inside these ranges and needn't reach their ends.
All inputs are finite; a program needn't handle non-finite values.
Results may differ from the reference program's by a relative error of at most 0.0043.
Values may be sent and summed in bfloat16 or wider, within the bound.
A program may use at most 128 MiB of HBM per device.

```python
import math
import jax
import jax.numpy as jnp
from jax import lax

LEV = 4
TIME = 32
TAPERS = 12
FREQS = 2
NLON = 384
NLAT = 512
ROWS = 1572864


def draw_winds(key, part):
    subkeys = jax.random.split(key, 3)
    shape = (2, TIME, LEV, NLON, NLAT)
    noise = jax.random.truncated_normal(subkeys[0], -4.0, 4.0, shape, jnp.float32)
    cell_scale = jnp.exp(jax.random.uniform(subkeys[1], (2, 1, LEV, NLON, NLAT), jnp.float32) * math.log(10.0))
    time_scale = jnp.exp(jax.random.uniform(subkeys[2], (2, TIME, 1, 1, 1), jnp.float32) * math.log(10.0))
    lon_ramp = 1.0 + 2.0 * jnp.arange(NLON, dtype=jnp.float32) / NLON
    return (noise * cell_scale * time_scale * lon_ramp[:, None] / 20.0).astype(jnp.bfloat16)


def setup_inputs(seed: int = 0) -> dict:
    key_of = jax.random.split(jax.random.key(seed), 2)
    winds = draw_winds(jax.random.fold_in(key_of[1], 71), 0)
    return dict(winds=winds)


def taper_table(times, tapers, freqs):
    times_f = jnp.arange(times, dtype=jnp.float32)
    order_k = jnp.arange(tapers, dtype=jnp.float32)
    weights = math.sqrt(2.0 / (times + 1)) * jnp.sin(math.pi * (order_k[:, None] + 1.0) * (times_f[None, :] + 1.0) / (times + 1))
    blocks = []
    for which in range(freqs):
        phases = 2.0 * math.pi * (7 + 2 * which) * times_f / times
        real_part = weights * jnp.cos(phases)[None, :]
        imag_part = -weights * jnp.sin(phases)[None, :]
        blocks.append(jnp.stack([real_part, imag_part], axis=1).reshape(2 * tapers, times))
    return jnp.concatenate(blocks, axis=0).astype(jnp.bfloat16)

def stencil(lon_pad, lat_pad, cos_lat, step_lon, step_lat):
    along_lon = (lon_pad[..., 2:, :].astype(jnp.float32) - lon_pad[..., :-2, :].astype(jnp.float32)) / (2.0 * step_lon)
    fluxes = lat_pad.astype(jnp.float32) * cos_lat
    along_lat = (fluxes[..., 2:] - fluxes[..., :-2]) / (2.0 * step_lat)
    middle = cos_lat[1:-1]
    vorticity = (along_lon[1] - along_lat[0]) / middle
    divergence = (along_lon[0] + along_lat[1]) / middle
    return jnp.stack([vorticity, divergence]).astype(jnp.bfloat16)

def reference(winds):
    step_lon = 2.0 * math.pi / NLON
    step_lat = 2.6 / NLAT
    lat_rows = jnp.arange(NLAT + 2, dtype=jnp.float32) - 1.0
    cos_lat = jnp.cos(-1.3 + (lat_rows + 0.5) * step_lat)
    table = taper_table(TIME, TAPERS, FREQS).astype(jnp.float32)

    def one_level(level_winds):
        lon_pad = jnp.concatenate([level_winds[..., -1:, :], level_winds, level_winds[..., :1, :]], axis=-2)
        zeros = jnp.zeros(level_winds.shape[:-1] + (1,), level_winds.dtype)
        lat_pad = jnp.concatenate([zeros, level_winds, zeros], axis=-1)
        fields = stencil(lon_pad, lat_pad, cos_lat, step_lon, step_lat)
        return jnp.einsum('ct,stxy->csxy', table, fields.astype(jnp.float32), precision=lax.Precision.HIGHEST)
    per_level = lax.map(one_level, jnp.moveaxis(winds, 2, 0))
    snapshots = jnp.moveaxis(per_level, 0, 2)
    columns = snapshots.reshape(FREQS, 2 * TAPERS, -1)
    gram = jnp.einsum('far,fbr->fab', columns, columns, precision=lax.Precision.HIGHEST) / ROWS
    factor = jnp.linalg.cholesky(gram)
    basis = jax.scipy.linalg.solve_triangular(factor, columns, lower=True)
    return basis.reshape(2 * FREQS * TAPERS, 2, LEV, NLON, NLAT)
```

```python
import functools
import math

import jax
import jax.numpy as jnp
import ml_dtypes
import numpy as np
from jax import lax
from jax.experimental import pallas as pl
from jax.experimental.pallas import tpu as pltpu
from jax.sharding import PartitionSpec as P

TIME = 32
TAPERS = 12
FREQS = 2
COLS = 2 * TAPERS
ALL = FREQS * COLS
SUB = 8
LANES = 128
PITCH = 64
LEAD = 8
CHUNKS = 4
MESH = pl.DeviceIdType.MESH
F32 = jnp.float32
BF16 = jnp.bfloat16


def taper_table():
    t = np.arange(TIME, dtype=np.float64)
    k = np.arange(TAPERS, dtype=np.float64)
    weights = math.sqrt(2.0 / (TIME + 1)) * np.sin(
        math.pi * (k[:, None] + 1.0) * (t[None, :] + 1.0) / (TIME + 1)
    )
    blocks = []
    for which in range(FREQS):
        phases = 2.0 * math.pi * (7 + 2 * which) * t / TIME
        pair = np.stack([weights * np.cos(phases), -weights * np.sin(phases)], axis=1)
        blocks.append(pair.reshape(COLS, TIME))
    return np.concatenate(blocks, axis=0).astype(np.float32).astype(ml_dtypes.bfloat16)


def lat_coefficients(grid_lon, grid_lat, bands):
    step_lon = 2.0 * math.pi / grid_lon
    step_lat = 2.6 / grid_lat
    cos_lat = np.cos(-1.3 + (np.arange(-1, grid_lat + 1) + 0.5) * step_lat)
    middle = cos_lat[1:-1]
    rows = np.stack(
        [
            1.0 / (2.0 * step_lon * middle),
            cos_lat[2:] / (2.0 * step_lat * middle),
            cos_lat[:-2] / (2.0 * step_lat * middle),
        ]
    ).astype(np.float32)
    rows = rows.reshape(3, bands, 1, LANES).transpose(1, 0, 2, 3)
    return np.broadcast_to(rows, (bands, 3, SUB, LANES)).copy()


def split(value, parts):
    pieces = []
    for _ in range(parts):
        piece = value.astype(BF16)
        pieces.append(piece)
        value = value - piece.astype(F32)
    return pieces


def iota(shape, dim):
    return lax.broadcasted_iota(jnp.int32, shape, dim)


def dot(a, b):
    return jnp.dot(a, b, preferred_element_type=F32)


def fields_kernel(
    n_lon, n_lat, levels, lon_cells, rows_total,
    winds, coef, table3, table_t, table_aug,
    x_out, mix_out,
    raw, padded, x_buf, pbuf, from_left, from_right, edges, row_first, row_last,
    row_prev, row_next, gram, mine, lon_slots, band, lat_slots,
    in_sem, out_sem, halo_send, halo_recv, lon_send, lon_recv, lat_send, lat_recv,
):
    lon = lax.axis_index("lon")
    lat = lax.axis_index("lat")
    groups = lon_cells // SUB
    blocks = 2 * TIME * levels
    per = 2 * TIME // CHUNKS
    cells = levels * lon_cells

    def load(c):
        part = pl.ds(c * per, per)
        return pltpu.make_async_copy(winds.at[part], raw.at[part], in_sem.at[c])

    for c in range(CHUNKS):
        load(c).start()
    from_left[...] = jnp.zeros_like(from_left)
    from_right[...] = jnp.zeros_like(from_right)

    barrier = pltpu.get_barrier_semaphore()
    for d in range(1, n_lon):
        pl.semaphore_signal(
            barrier, inc=1, device_id=(lax.rem(lon + d, n_lon), lat), device_id_type=MESH
        )
    for d in range(1, n_lat):
        pl.semaphore_signal(
            barrier, inc=1, device_id=(lon, lax.rem(lat + d, n_lat)), device_id_type=MESH
        )

    lane_c = iota((cells, LANES), 1)

    def widen(q, packed):
        x = raw[q].astype(F32)
        for l in range(levels):
            start = pl.multiple_of((q * levels + l) * PITCH + LEAD, 8)
            padded[pl.ds(start, lon_cells), :] = x[l * lon_cells:(l + 1) * lon_cells]
        turned = pltpu.roll(x, 2 * q + 1, 1)
        return jnp.where(lane_c // 2 == q, turned, packed)

    packed = jnp.zeros((cells, LANES), F32)
    for c in range(CHUNKS):
        load(c).wait()
        packed = lax.fori_loop(c * per, (c + 1) * per, widen, packed)
    pbuf[...] = packed.astype(BF16)

    pl.semaphore_wait(barrier, n_lon + n_lat - 2)

    def remote(src, dst, send, recv, device):
        return pltpu.make_async_remote_copy(
            src_ref=src, dst_ref=dst, send_sem=send, recv_sem=recv,
            device_id=device, device_id_type=MESH,
        )

    up = remote(pbuf, from_left, halo_send.at[0], halo_recv.at[0], (lon, lax.rem(lat + 1, n_lat)))
    down = remote(
        pbuf, from_right, halo_send.at[1], halo_recv.at[1], (lon, lax.rem(lat + n_lat - 1, n_lat))
    )
    pl.when(lat < n_lat - 1)(lambda: up.start())
    pl.when(lat > 0)(lambda: down.start())

    row_first[...] = padded[pl.ds(LEAD, blocks, stride=PITCH), :].astype(BF16)
    row_last[...] = padded[pl.ds(LEAD + lon_cells - 1, blocks, stride=PITCH), :].astype(BF16)
    east = remote(
        row_last, row_prev, halo_send.at[2], halo_recv.at[2], (lax.rem(lon + 1, n_lon), lat)
    )
    west = remote(
        row_first, row_next, halo_send.at[3], halo_recv.at[3], (lax.rem(lon + n_lon - 1, n_lon), lat)
    )
    east.start()
    west.start()

    pl.when(lat > 0)(lambda: up.wait_recv())
    pl.when(lat < n_lat - 1)(lambda: down.wait_recv())
    edges[...] = jnp.where(
        lane_c % 2 == 0,
        from_left[...].astype(F32),
        pltpu.roll(from_right[...].astype(F32), LANES - 2, 1),
    )
    east.wait_recv()
    padded[pl.ds(LEAD - 1, blocks, stride=PITCH), :] = row_prev[...].astype(F32)
    west.wait_recv()
    padded[pl.ds(LEAD + lon_cells, blocks, stride=PITCH), :] = row_next[...].astype(F32)

    batch = 4
    lane = iota((batch * SUB, LANES), 1)
    first = lane == 0
    last = lane == LANES - 1
    along = jnp.concatenate([coef[lat, 0]] * batch, axis=0)
    ahead = jnp.concatenate([coef[lat, 1]] * batch, axis=0)
    behind = jnp.concatenate([coef[lat, 2]] * batch, axis=0)

    def one_group(step, carry):
        level = step // groups
        group = lax.rem(step, groups)
        edge = edges[pl.ds(pl.multiple_of(step * SUB, SUB), SUB), :]
        for t0 in range(0, TIME, batch):
            d_lon, d_lat = [], []
            for comp in range(2):
                def rows(shift):
                    parts = []
                    for t in range(t0, t0 + batch):
                        q = comp * TIME + t
                        start = (q * levels + level) * PITCH + LEAD + group * SUB + shift
                        parts.append(padded[pl.ds(start, SUB), :])
                    return jnp.concatenate(parts, axis=0)

                d_lon.append((rows(1) - rows(-1)) * along)
                center = rows(0)
                halo = jnp.concatenate(
                    [
                        pltpu.roll(edge, (LANES - 2 * (comp * TIME + t)) % LANES, 1)
                        for t in range(t0, t0 + batch)
                    ],
                    axis=0,
                )
                nxt = jnp.where(last, halo, pltpu.roll(center, LANES - 1, 1))
                prv = jnp.where(first, halo, pltpu.roll(center, 1, 1))
                d_lat.append(nxt * ahead - prv * behind)
            here = pl.ds(t0 * SUB, batch * SUB)
            vort_at = pl.ds(pl.multiple_of(step * LANES, LANES), LANES)
            div_at = pl.ds(pl.multiple_of((step + levels * groups) * LANES, LANES), LANES)
            x_buf[here, vort_at] = (d_lon[1] - d_lat[0]).astype(BF16)
            x_buf[here, div_at] = (d_lon[0] + d_lat[1]).astype(BF16)
        return carry

    lax.fori_loop(0, levels * groups, one_group, 0)
    store = pltpu.make_async_copy(x_buf, x_out, out_sem)
    store.start()

    wide = 8 * LANES
    side = TIME * SUB

    def add_gram(c, carry):
        x = x_buf[:, pl.ds(pl.multiple_of(c * wide, wide), wide)]
        term = lax.dot_general(x, x, (((1,), (1,)), ((), ())), preferred_element_type=F32)
        gram[...] = gram[...] + term
        return carry

    gram[...] = jnp.zeros_like(gram)
    lax.fori_loop(0, 2 * levels * groups * LANES // wide, add_gram, 0)
    same = iota((side, side), 0) % SUB == iota((side, side), 1) % SUB
    by_time = jnp.sum(jnp.where(same, gram[...], 0.0).reshape(TIME, SUB, side), axis=1)
    fold = (iota((side, LANES), 0) // SUB == iota((side, LANES), 1)).astype(F32).astype(BF16)
    folded = dot(jnp.concatenate(split(by_time, 3), axis=0), fold)
    times = folded[:TIME] + folded[TIME:2 * TIME] + folded[2 * TIME:]
    tile = times[:SUB]
    for a in range(1, TIME // SUB):
        tile = tile + pltpu.roll(times[a * SUB:(a + 1) * SUB], a * TIME, 1)
    mine[...] = tile

    lon_copies = [
        remote(mine, lon_slots.at[d - 1], lon_send.at[d - 1], lon_recv.at[d - 1],
               (lax.rem(lon + d, n_lon), lat))
        for d in range(1, n_lon)
    ]
    for copy in lon_copies:
        copy.start()
    total = mine[...]
    for d, copy in enumerate(lon_copies):
        copy.wait_recv()
        total = total + lon_slots[d]
    band[...] = total
    lat_copies = [
        remote(band, lat_slots.at[d - 1], lat_send.at[d - 1], lat_recv.at[d - 1],
               (lon, lax.rem(lat + d, n_lat)))
        for d in range(1, n_lat)
    ]
    for copy in lat_copies:
        copy.start()
    total = band[...]
    for d, copy in enumerate(lat_copies):
        copy.wait_recv()
        total = total + lat_slots[d]

    total = total * (1.0 / rows_total)
    square = jnp.concatenate(
        [total] + [pltpu.roll(total, LANES - a * TIME, 1) for a in range(1, TIME // SUB)], axis=0
    )
    half = dot(table3[...], jnp.concatenate(split(square, 3), axis=0))
    full = dot(jnp.concatenate(split(half, 3), axis=0), table_t[...])
    full = full[:ALL] + full[ALL:2 * ALL] + full[2 * ALL:]
    aug = jnp.where(iota((ALL, LANES), 1) < 64, full, table_aug[...])
    row = iota((COLS, 1), 0)
    lane_a = iota((COLS, LANES), 1)
    parts = [aug[:COLS], aug[COLS:]]
    for k in range(COLS):
        for f in range(FREQS):
            a = parts[f]
            at = f * COLS + k
            pivot = a[k:k + 1, :]
            scale = jnp.where(row > k, a[:, at:at + 1] / pivot[:, at:at + 1], 0.0)
            parts[f] = a - scale * pivot
    rows_done = []
    for f in range(FREQS):
        on_diag = lane_a == iota((COLS, LANES), 0) + f * COLS
        diag = jnp.sum(jnp.where(on_diag, parts[f], 0.0), axis=1, keepdims=True)
        rows_done.append(parts[f] / jnp.sqrt(diag))
    mix = jnp.concatenate(rows_done, axis=0)
    spread = (iota((LANES, side), 0) - 64 == iota((LANES, side), 1) // SUB).astype(F32).astype(BF16)
    wide_mix = dot(jnp.concatenate(split(mix, 2), axis=0), spread)
    tall = jnp.broadcast_to(wide_mix[:, None, :], (2 * ALL, SUB, side)).reshape(2 * ALL * SUB, side)
    keep = iota(tall.shape, 0) % SUB == iota(tall.shape, 1) % SUB
    tall = jnp.where(keep, tall, 0.0).astype(BF16)
    mix_out[:, :side] = tall[:ALL * SUB]
    mix_out[:, side:] = tall[ALL * SUB:]

    pl.when(lat < n_lat - 1)(lambda: up.wait_send())
    pl.when(lat > 0)(lambda: down.wait_send())
    for copy in [east, west] + lon_copies + lat_copies:
        copy.wait_send()
    store.wait()


def basis_kernel(mix, x, out):
    lon_cells = out.shape[2]
    weights = mix[...]
    for g in range(0, lon_cells // SUB, 2):
        part = x[:, g * LANES:(g + 2) * LANES]
        res = dot(weights, jnp.concatenate([part, part], axis=0))
        for h in range(2):
            cols = res[:, h * LANES:(h + 1) * LANES].reshape(ALL, SUB, LANES)
            out[:, 0, (g + h) * SUB:(g + h + 1) * SUB, :] = cols


def body(n_lon, n_lat, winds):
    _, times, levels, lon_cells, lat_cells = winds.shape
    cells = levels * lon_cells
    columns = 2 * cells // SUB * LANES
    side = TIME * SUB
    table = taper_table()
    table3 = np.concatenate([table] * 3, axis=1)
    table_t = np.zeros((LANES, LANES), ml_dtypes.bfloat16)
    table_t[:TIME, :ALL] = table.T
    table_aug = np.zeros((ALL, LANES), np.float32)
    table_aug[:, 64:64 + TIME] = table.astype(np.float32)
    coef = lat_coefficients(n_lon * lon_cells, n_lat * lat_cells, n_lat)
    rows_total = 2 * levels * lon_cells * n_lon * lat_cells * n_lat
    vmem = pl.BlockSpec(memory_space=pltpu.VMEM)
    anywhere = pl.BlockSpec(memory_space=pl.ANY)
    blocks = 2 * TIME * levels
    dma = pltpu.SemaphoreType.DMA
    x, mix = pl.pallas_call(
        functools.partial(fields_kernel, n_lon, n_lat, levels, lon_cells, rows_total),
        out_shape=(
            jax.ShapeDtypeStruct((side, columns), BF16),
            jax.ShapeDtypeStruct((ALL * SUB, 2 * side), BF16),
        ),
        in_specs=[anywhere, vmem, vmem, vmem, vmem],
        out_specs=(anywhere, vmem),
        scratch_shapes=[
            pltpu.VMEM((2 * TIME, cells, LANES), BF16),
            pltpu.VMEM((blocks * PITCH, LANES), F32),
            pltpu.VMEM((side, columns), BF16),
            pltpu.VMEM((cells, LANES), BF16),
            pltpu.VMEM((cells, LANES), BF16),
            pltpu.VMEM((cells, LANES), BF16),
            pltpu.VMEM((cells, LANES), F32),
            pltpu.VMEM((blocks, LANES), BF16),
            pltpu.VMEM((blocks, LANES), BF16),
            pltpu.VMEM((blocks, LANES), BF16),
            pltpu.VMEM((blocks, LANES), BF16),
            pltpu.VMEM((side, side), F32),
            pltpu.VMEM((SUB, LANES), F32),
            pltpu.VMEM((n_lon - 1, SUB, LANES), F32),
            pltpu.VMEM((SUB, LANES), F32),
            pltpu.VMEM((n_lat - 1, SUB, LANES), F32),
            dma((CHUNKS,)),
            dma(()),
            dma((4,)),
            dma((4,)),
            dma((n_lon - 1,)),
            dma((n_lon - 1,)),
            dma((n_lat - 1,)),
            dma((n_lat - 1,)),
        ],
        compiler_params=pltpu.CompilerParams(
            collective_id=0, has_side_effects=True, vmem_limit_bytes=40 * 2**20
        ),
        name="fields",
    )(
        winds.reshape(2 * TIME, cells, LANES),
        jnp.asarray(coef),
        jnp.asarray(table3),
        jnp.asarray(table_t),
        jnp.asarray(table_aug),
    )
    width = lon_cells // SUB * LANES
    basis = pl.pallas_call(
        basis_kernel,
        grid=(2 * levels,),
        out_shape=jax.ShapeDtypeStruct((ALL, 2 * levels, lon_cells, LANES), F32),
        in_specs=[
            pl.BlockSpec((ALL * SUB, 2 * side), lambda i: (0, 0)),
            pl.BlockSpec((side, width), lambda i: (0, i)),
        ],
        out_specs=pl.BlockSpec((ALL, 1, lon_cells, LANES), lambda i: (0, i, 0, 0)),
        compiler_params=pltpu.CompilerParams(vmem_limit_bytes=40 * 2**20),
        name="basis",
    )(mix, x)
    return basis.reshape(ALL, 2, levels, lon_cells, lat_cells)


def solution(mesh):
    spec = P(None, None, None, "lon", "lat")
    run = functools.partial(body, mesh.shape["lon"], mesh.shape["lat"])
    return jax.shard_map(run, mesh=mesh, in_specs=(spec,), out_specs=spec, check_vma=False)
```

```python
import functools
import math

import jax
import jax.numpy as jnp
import ml_dtypes
import numpy as np
from jax import lax
from jax.experimental import pallas as pl
from jax.experimental.pallas import tpu as pltpu
from jax.sharding import PartitionSpec as P

TIME = 32
TAPERS = 12
FREQS = 2
COLS = 2 * TAPERS
ALL = FREQS * COLS
SUB = 8
LANES = 128
PITCH = 56
LEAD = 8
CHUNKS = 4
MESH = pl.DeviceIdType.MESH
F32 = jnp.float32
BF16 = jnp.bfloat16


def taper_table():
    t = np.arange(TIME, dtype=np.float64)
    k = np.arange(TAPERS, dtype=np.float64)
    weights = math.sqrt(2.0 / (TIME + 1)) * np.sin(
        math.pi * (k[:, None] + 1.0) * (t[None, :] + 1.0) / (TIME + 1)
    )
    blocks = []
    for which in range(FREQS):
        phases = 2.0 * math.pi * (7 + 2 * which) * t / TIME
        pair = np.stack([weights * np.cos(phases), -weights * np.sin(phases)], axis=1)
        blocks.append(pair.reshape(COLS, TIME))
    return np.concatenate(blocks, axis=0).astype(np.float32).astype(ml_dtypes.bfloat16)


def lat_coefficients(grid_lon, grid_lat, bands):
    step_lon = 2.0 * math.pi / grid_lon
    step_lat = 2.6 / grid_lat
    cos_lat = np.cos(-1.3 + (np.arange(-1, grid_lat + 1) + 0.5) * step_lat)
    middle = cos_lat[1:-1]
    rows = np.stack(
        [
            1.0 / (2.0 * step_lon * middle),
            cos_lat[2:] / (2.0 * step_lat * middle),
            cos_lat[:-2] / (2.0 * step_lat * middle),
        ]
    ).astype(np.float32)
    rows = rows.reshape(3, bands, 1, LANES).transpose(1, 0, 2, 3)
    return np.broadcast_to(rows, (bands, 3, SUB, LANES)).copy()


def split(value, parts):
    pieces = []
    for _ in range(parts):
        piece = value.astype(BF16)
        pieces.append(piece)
        value = value - piece.astype(F32)
    return pieces


def iota(shape, dim):
    return lax.broadcasted_iota(jnp.int32, shape, dim)


def dot(a, b):
    return jnp.dot(a, b, preferred_element_type=F32)


def fields_kernel(
    n_lon, n_lat, levels, lon_cells, rows_total,
    winds, consts,
    x_out, mix_out,
    coef, tables, raw, padded, x_buf, pbuf, from_left, from_right, edges, row_first, row_last,
    row_prev, row_next, gram, mine, lon_slots, band, lat_slots,
    in_sem, const_sem, out_sem, halo_send, halo_recv, lon_send, lon_recv, lat_send, lat_recv,
):
    lon = lax.axis_index("lon")
    lat = lax.axis_index("lat")
    groups = lon_cells // SUB
    blocks = 2 * TIME * levels
    per = 2 * TIME // CHUNKS
    cells = levels * lon_cells

    def load(c):
        part = pl.ds(c * per, per)
        return pltpu.make_async_copy(winds.at[part], raw.at[part], in_sem.at[c])

    for c in range(CHUNKS):
        load(c).start()
    band_rows = 3 * SUB
    get_coef = pltpu.make_async_copy(
        consts.at[pl.ds(pl.multiple_of(lat * band_rows, 8), band_rows)], coef, const_sem.at[0]
    )
    get_tables = pltpu.make_async_copy(
        consts.at[pl.ds(n_lat * band_rows, tables.shape[0])], tables, const_sem.at[1]
    )
    get_coef.start()
    get_tables.start()
    from_left[...] = jnp.zeros_like(from_left)
    from_right[...] = jnp.zeros_like(from_right)

    barrier = pltpu.get_barrier_semaphore()
    for d in range(1, n_lon):
        pl.semaphore_signal(
            barrier, inc=1, device_id=(lax.rem(lon + d, n_lon), lat), device_id_type=MESH
        )
    for d in range(1, n_lat):
        pl.semaphore_signal(
            barrier, inc=1, device_id=(lon, lax.rem(lat + d, n_lat)), device_id_type=MESH
        )

    pair = iota((SUB, LANES), 1) >> 1

    def widen(q, packed):
        x = raw[q].astype(F32)
        for l in range(levels):
            start = pl.multiple_of((q * levels + l) * PITCH + LEAD, 8)
            padded[pl.ds(start, lon_cells), :] = x[l * lon_cells:(l + 1) * lon_cells]
        turned = pltpu.roll(x, 2 * q + 1, 1).reshape(cells // SUB, SUB, LANES)
        return jnp.where((pair == q)[None], turned, packed)

    packed = jnp.zeros((cells // SUB, SUB, LANES), F32)
    for c in range(CHUNKS):
        load(c).wait()
        packed = lax.fori_loop(c * per, (c + 1) * per, widen, packed)
    pbuf[...] = packed.reshape(cells, LANES).astype(BF16)

    pl.semaphore_wait(barrier, n_lon + n_lat - 2)

    def remote(src, dst, send, recv, device):
        return pltpu.make_async_remote_copy(
            src_ref=src, dst_ref=dst, send_sem=send, recv_sem=recv,
            device_id=device, device_id_type=MESH,
        )

    up = remote(pbuf, from_left, halo_send.at[0], halo_recv.at[0], (lon, lax.rem(lat + 1, n_lat)))
    down = remote(
        pbuf, from_right, halo_send.at[1], halo_recv.at[1], (lon, lax.rem(lat + n_lat - 1, n_lat))
    )
    pl.when(lat < n_lat - 1)(lambda: up.start())
    pl.when(lat > 0)(lambda: down.start())

    row_first[...] = padded[pl.ds(LEAD, blocks, stride=PITCH), :].astype(BF16)
    row_last[...] = padded[pl.ds(LEAD + lon_cells - 1, blocks, stride=PITCH), :].astype(BF16)
    east = remote(
        row_last, row_prev, halo_send.at[2], halo_recv.at[2], (lax.rem(lon + 1, n_lon), lat)
    )
    west = remote(
        row_first, row_next, halo_send.at[3], halo_recv.at[3], (lax.rem(lon + n_lon - 1, n_lon), lat)
    )
    east.start()
    west.start()

    pl.when(lat > 0)(lambda: up.wait_recv())
    pl.when(lat < n_lat - 1)(lambda: down.wait_recv())
    edges[...] = jnp.where(
        iota((cells, LANES), 1) % 2 == 0,
        from_left[...].astype(F32),
        pltpu.roll(from_right[...].astype(F32), LANES - 2, 1),
    )
    east.wait_recv()
    padded[pl.ds(LEAD - 1, blocks, stride=PITCH), :] = row_prev[...].astype(F32)
    west.wait_recv()
    padded[pl.ds(LEAD + lon_cells, blocks, stride=PITCH), :] = row_next[...].astype(F32)

    batch = 4
    lane = iota((batch * SUB, LANES), 1)
    first = lane == 0
    last = lane == LANES - 1
    get_coef.wait()
    along, ahead, behind = (
        jnp.concatenate([coef[i * SUB:(i + 1) * SUB, :]] * batch, axis=0) for i in range(3)
    )

    def one_group(level, group):
        step = level * groups + group
        base = level * PITCH + group * SUB
        edge = edges[pl.ds(pl.multiple_of(step * SUB, SUB), SUB), :]
        for t0 in range(0, TIME, batch):
            d_lon, d_lat = [], []
            for comp in range(2):
                def rows(shift):
                    parts = []
                    for t in range(t0, t0 + batch):
                        offset = (comp * TIME + t) * levels * PITCH + LEAD + shift
                        parts.append(padded[pl.ds(base + offset, SUB), :])
                    return jnp.concatenate(parts, axis=0)

                d_lon.append((rows(1) - rows(-1)) * along)
                center = rows(0)
                halo = jnp.concatenate(
                    [
                        pltpu.roll(edge, (LANES - 2 * (comp * TIME + t)) % LANES, 1)
                        for t in range(t0, t0 + batch)
                    ],
                    axis=0,
                )
                nxt = jnp.where(last, halo, pltpu.roll(center, LANES - 1, 1))
                prv = jnp.where(first, halo, pltpu.roll(center, 1, 1))
                d_lat.append(nxt * ahead - prv * behind)
            here = pl.ds(t0 * SUB, batch * SUB)
            vort_at = pl.ds(pl.multiple_of(step * LANES, LANES), LANES)
            div_at = pl.ds(pl.multiple_of((step + levels * groups) * LANES, LANES), LANES)
            x_buf[here, vort_at] = (d_lon[1] - d_lat[0]).astype(BF16)
            x_buf[here, div_at] = (d_lon[0] + d_lat[1]).astype(BF16)

    @pl.loop(0, levels)
    def _(level):
        @pl.loop(0, groups)
        def _(group):
            one_group(level, group)

    store = pltpu.make_async_copy(x_buf, x_out, out_sem)
    store.start()

    wide = 8 * LANES
    side = TIME * SUB

    def add_gram(c, carry):
        x = x_buf[:, pl.ds(pl.multiple_of(c * wide, wide), wide)]
        term = lax.dot_general(x, x, (((1,), (1,)), ((), ())), preferred_element_type=F32)
        gram[...] = gram[...] + term
        return carry

    gram[...] = jnp.zeros_like(gram)
    lax.fori_loop(0, 2 * levels * groups * LANES // wide, add_gram, 0)
    same = iota((side, side), 0) % SUB == iota((side, side), 1) % SUB
    by_time = jnp.sum(jnp.where(same, gram[...], 0.0).reshape(TIME, SUB, side), axis=1)
    fold = (iota((side, LANES), 0) // SUB == iota((side, LANES), 1)).astype(F32).astype(BF16)
    folded = dot(jnp.concatenate(split(by_time, 3), axis=0), fold)
    times = folded[:TIME] + folded[TIME:2 * TIME] + folded[2 * TIME:]
    tile = times[:SUB]
    for a in range(1, TIME // SUB):
        tile = tile + pltpu.roll(times[a * SUB:(a + 1) * SUB], a * TIME, 1)
    mine[...] = tile

    lon_copies = [
        remote(mine, lon_slots.at[d - 1], lon_send.at[d - 1], lon_recv.at[d - 1],
               (lax.rem(lon + d, n_lon), lat))
        for d in range(1, n_lon)
    ]
    for copy in lon_copies:
        copy.start()
    total = mine[...]
    for d, copy in enumerate(lon_copies):
        copy.wait_recv()
        total = total + lon_slots[d]
    band[...] = total
    lat_copies = [
        remote(band, lat_slots.at[d - 1], lat_send.at[d - 1], lat_recv.at[d - 1],
               (lon, lax.rem(lat + d, n_lat)))
        for d in range(1, n_lat)
    ]
    for copy in lat_copies:
        copy.start()
    total = band[...]
    for d, copy in enumerate(lat_copies):
        copy.wait_recv()
        total = total + lat_slots[d]

    total = total * (1.0 / rows_total)
    square = jnp.concatenate(
        [total] + [pltpu.roll(total, LANES - a * TIME, 1) for a in range(1, TIME // SUB)], axis=0
    )
    get_tables.wait()
    table3 = tables[:ALL, :].astype(BF16)
    table_aug = tables[ALL:2 * ALL, :]
    table_t = tables[2 * ALL:, :].astype(BF16)
    stacked = split(square, 3) + [jnp.zeros((TIME, LANES), BF16)]
    half = dot(table3, jnp.concatenate(stacked, axis=0))
    full = dot(jnp.concatenate(split(half, 3), axis=0), table_t)
    full = full[:ALL] + full[ALL:2 * ALL] + full[2 * ALL:]
    aug = jnp.where(iota((ALL, LANES), 1) < 64, full, table_aug)
    row = iota((COLS, LANES), 0)
    lane_a = iota((COLS, LANES), 1)
    parts = [aug[:COLS], aug[COLS:]]
    panel = 8
    for start in range(0, COLS, panel):
        columns = [
            [
                jnp.broadcast_to(parts[f][:, at:at + 1], (COLS, LANES))
                for at in range(f * COLS + start, f * COLS + start + panel)
            ]
            for f in range(FREQS)
        ]
        for j in range(panel):
            k = start + j
            for f in range(FREQS):
                cols = columns[f]
                scale = jnp.where(row > k, cols[j] * (1.0 / cols[j][k:k + 1, :]), 0.0)
                for i in range(j + 1, panel):
                    cols[i] = cols[i] - scale * cols[i][k:k + 1, :]
                parts[f] = parts[f] - scale * parts[f][k:k + 1, :]
    rows_done = []
    for f in range(FREQS):
        on_diag = lane_a == iota((COLS, LANES), 0) + f * COLS
        diag = jnp.sum(jnp.where(on_diag, parts[f], 0.0), axis=1, keepdims=True)
        rows_done.append(parts[f] / jnp.sqrt(diag))
    mix = jnp.concatenate(rows_done, axis=0)
    spread = (iota((LANES, side), 0) - 64 == iota((LANES, side), 1) // SUB).astype(F32).astype(BF16)
    wide_mix = dot(jnp.concatenate(split(mix, 2), axis=0), spread)
    tall = jnp.broadcast_to(wide_mix[:, None, :], (2 * ALL, SUB, side)).reshape(2 * ALL * SUB, side)
    keep = iota(tall.shape, 0) % SUB == iota(tall.shape, 1) % SUB
    tall = jnp.where(keep, tall, 0.0).astype(BF16)
    mix_out[:, :side] = tall[:ALL * SUB]
    mix_out[:, side:] = tall[ALL * SUB:]

    pl.when(lat < n_lat - 1)(lambda: up.wait_send())
    pl.when(lat > 0)(lambda: down.wait_send())
    for copy in [east, west] + lon_copies + lat_copies:
        copy.wait_send()
    store.wait()


def basis_kernel(mix, x, out, mix_buf, x_buf, out_buf, mix_sem, x_sem, out_sem):
    slabs, lon_cells = out.shape[1], out.shape[2]
    width = lon_cells // SUB * LANES
    pairs = lon_cells // (2 * SUB)
    get_mix = pltpu.make_async_copy(mix, mix_buf, mix_sem)
    get_mix.start()

    def get_x(i):
        part = pl.ds(pl.multiple_of(i * width, LANES), width)
        return pltpu.make_async_copy(x.at[:, part], x_buf.at[:, part], x_sem.at[i])

    def put(i, g):
        part = (slice(None), i, pl.ds(g * 2 * SUB, 2 * SUB))
        return pltpu.make_async_copy(out_buf.at[part], out.at[part], out_sem.at[i, g])

    for i in range(slabs):
        get_x(i).start()
    get_mix.wait()

    @pl.loop(0, slabs)
    def _(i):
        get_x(i).wait()
        for g in range(pairs):
            at = pl.multiple_of(i * width + g * 2 * LANES, LANES)
            part = x_buf[:, pl.ds(at, 2 * LANES)]
            res = dot(mix_buf[...], jnp.concatenate([part, part], axis=0))
            for h in range(2):
                cols = res[:, h * LANES:(h + 1) * LANES].reshape(ALL, SUB, LANES)
                out_buf[:, i, (2 * g + h) * SUB:(2 * g + h + 1) * SUB, :] = cols
            put(i, g).start()

    @pl.loop(0, slabs)
    def _(i):
        for g in range(pairs):
            put(i, g).wait()


def body(n_lon, n_lat, winds):
    _, times, levels, lon_cells, lat_cells = winds.shape
    cells = levels * lon_cells
    columns = 2 * cells // SUB * LANES
    side = TIME * SUB
    table = taper_table().astype(np.float32)
    used = n_lat * 3 * SUB + 2 * ALL + LANES
    consts = np.zeros((8192, LANES), np.float32)
    coef = lat_coefficients(n_lon * lon_cells, n_lat * lat_cells, n_lat)
    consts[:n_lat * 3 * SUB] = coef.reshape(-1, LANES)
    tables = consts[n_lat * 3 * SUB:used]
    tables[:ALL, :3 * TIME] = np.concatenate([table] * 3, axis=1)
    tables[ALL:2 * ALL, 64:64 + TIME] = table
    tables[2 * ALL:2 * ALL + TIME, :ALL] = table.T
    rows_total = 2 * levels * lon_cells * n_lon * lat_cells * n_lat
    vmem = pl.BlockSpec(memory_space=pltpu.VMEM)
    anywhere = pl.BlockSpec(memory_space=pl.ANY)
    hbm = pl.BlockSpec(memory_space=pltpu.HBM)
    blocks = 2 * TIME * levels
    dma = pltpu.SemaphoreType.DMA
    x, mix = pl.pallas_call(
        functools.partial(fields_kernel, n_lon, n_lat, levels, lon_cells, rows_total),
        out_shape=(
            jax.ShapeDtypeStruct((side, columns), BF16),
            jax.ShapeDtypeStruct((ALL * SUB, 2 * side), BF16),
        ),
        in_specs=[hbm, hbm],
        out_specs=(anywhere, vmem),
        scratch_shapes=[
            pltpu.VMEM((3 * SUB, LANES), F32),
            pltpu.VMEM((2 * ALL + LANES, LANES), F32),
            pltpu.VMEM((2 * TIME, cells, LANES), BF16),
            pltpu.VMEM((blocks * PITCH + LEAD, LANES), F32),
            pltpu.VMEM((side, columns), BF16),
            pltpu.VMEM((cells, LANES), BF16),
            pltpu.VMEM((cells, LANES), BF16),
            pltpu.VMEM((cells, LANES), BF16),
            pltpu.VMEM((cells, LANES), F32),
            pltpu.VMEM((blocks, LANES), BF16),
            pltpu.VMEM((blocks, LANES), BF16),
            pltpu.VMEM((blocks, LANES), BF16),
            pltpu.VMEM((blocks, LANES), BF16),
            pltpu.VMEM((side, side), F32),
            pltpu.VMEM((SUB, LANES), F32),
            pltpu.VMEM((n_lon - 1, SUB, LANES), F32),
            pltpu.VMEM((SUB, LANES), F32),
            pltpu.VMEM((n_lat - 1, SUB, LANES), F32),
            dma((CHUNKS,)),
            dma((2,)),
            dma(()),
            dma((4,)),
            dma((4,)),
            dma((n_lon - 1,)),
            dma((n_lon - 1,)),
            dma((n_lat - 1,)),
            dma((n_lat - 1,)),
        ],
        compiler_params=pltpu.CompilerParams(
            collective_id=0, has_side_effects=True, vmem_limit_bytes=50 * 2**20
        ),
        name="fields",
    )(
        winds.reshape(2 * TIME, cells, LANES),
        jnp.asarray(consts),
    )
    basis = pl.pallas_call(
        basis_kernel,
        out_shape=jax.ShapeDtypeStruct((ALL, 2 * levels, lon_cells, LANES), F32),
        in_specs=[anywhere, anywhere],
        out_specs=hbm,
        scratch_shapes=[
            pltpu.VMEM((ALL * SUB, 2 * side), BF16),
            pltpu.VMEM((side, columns), BF16),
            pltpu.VMEM((ALL, 2 * levels, lon_cells, LANES), F32),
            dma(()),
            dma((2 * levels,)),
            dma((2 * levels, lon_cells // (2 * SUB))),
        ],
        compiler_params=pltpu.CompilerParams(vmem_limit_bytes=20 * 2**20),
        name="basis",
    )(mix, x)
    return basis.reshape(ALL, 2, levels, lon_cells, lat_cells)


def solution(mesh):
    spec = P(None, None, None, "lon", "lat")
    run = functools.partial(body, mesh.shape["lon"], mesh.shape["lat"])
    return jax.shard_map(run, mesh=mesh, in_specs=(spec,), out_specs=spec, check_vma=False)
```

```python
import functools
import math

import jax
import jax.numpy as jnp
import ml_dtypes
import numpy as np
from jax import lax
from jax.experimental import pallas as pl
from jax.experimental.pallas import tpu as pltpu
from jax.sharding import PartitionSpec as P

TIME = 32
TAPERS = 12
FREQS = 2
COLS = 2 * TAPERS
ALL = FREQS * COLS
SUB = 8
LANES = 128
PITCH = 56
LEAD = 8
CHUNKS = 4
MESH = pl.DeviceIdType.MESH
F32 = jnp.float32
BF16 = jnp.bfloat16


def taper_table():
    t = np.arange(TIME, dtype=np.float64)
    k = np.arange(TAPERS, dtype=np.float64)
    weights = math.sqrt(2.0 / (TIME + 1)) * np.sin(
        math.pi * (k[:, None] + 1.0) * (t[None, :] + 1.0) / (TIME + 1)
    )
    blocks = []
    for which in range(FREQS):
        phases = 2.0 * math.pi * (7 + 2 * which) * t / TIME
        pair = np.stack([weights * np.cos(phases), -weights * np.sin(phases)], axis=1)
        blocks.append(pair.reshape(COLS, TIME))
    return np.concatenate(blocks, axis=0).astype(np.float32).astype(ml_dtypes.bfloat16)


def lat_coefficients(grid_lon, grid_lat, bands):
    step_lon = 2.0 * math.pi / grid_lon
    step_lat = 2.6 / grid_lat
    cos_lat = np.cos(-1.3 + (np.arange(-1, grid_lat + 1) + 0.5) * step_lat)
    middle = cos_lat[1:-1]
    rows = np.stack(
        [
            1.0 / (2.0 * step_lon * middle),
            cos_lat[2:] / (2.0 * step_lat * middle),
            cos_lat[:-2] / (2.0 * step_lat * middle),
        ]
    ).astype(np.float32)
    rows = rows.reshape(3, bands, 1, LANES).transpose(1, 0, 2, 3)
    return np.broadcast_to(rows, (bands, 3, SUB, LANES)).copy()


def split(value, parts):
    pieces = []
    for _ in range(parts):
        piece = value.astype(BF16)
        pieces.append(piece)
        value = value - piece.astype(F32)
    return pieces


def iota(shape, dim):
    return lax.broadcasted_iota(jnp.int32, shape, dim)


def dot(a, b):
    return jnp.dot(a, b, preferred_element_type=F32)


def fields_kernel(
    n_lon, n_lat, levels, lon_cells, rows_total,
    winds, consts,
    x_out, mix_out,
    coef, tables, raw, padded, x_buf, pbuf, from_left, from_right, edges, row_first, row_last,
    row_prev, row_next, gram, mine, lon_slots, band, lat_slots,
    in_sem, const_sem, out_sem, halo_send, halo_recv, lon_send, lon_recv, lat_send, lat_recv,
):
    lon = lax.axis_index("lon")
    lat = lax.axis_index("lat")
    groups = lon_cells // SUB
    blocks = 2 * TIME * levels
    per = 2 * TIME // CHUNKS
    cells = levels * lon_cells

    def load(c):
        part = pl.ds(c * per, per)
        return pltpu.make_async_copy(winds.at[part], raw.at[part], in_sem.at[c])

    for c in range(CHUNKS):
        load(c).start()
    band_rows = 3 * SUB
    get_coef = pltpu.make_async_copy(
        consts.at[pl.ds(pl.multiple_of(lat * band_rows, 8), band_rows)], coef, const_sem.at[0]
    )
    get_tables = pltpu.make_async_copy(
        consts.at[pl.ds(n_lat * band_rows, tables.shape[0])], tables, const_sem.at[1]
    )
    get_coef.start()
    get_tables.start()
    from_left[...] = jnp.zeros_like(from_left)
    from_right[...] = jnp.zeros_like(from_right)

    barrier = pltpu.get_barrier_semaphore()
    for d in range(1, n_lon):
        pl.semaphore_signal(
            barrier, inc=1, device_id=(lax.rem(lon + d, n_lon), lat), device_id_type=MESH
        )
    for d in range(1, n_lat):
        pl.semaphore_signal(
            barrier, inc=1, device_id=(lon, lax.rem(lat + d, n_lat)), device_id_type=MESH
        )

    pair = iota((SUB, LANES), 1) >> 1

    def widen(q, packed):
        x = raw[q].astype(F32)
        for l in range(levels):
            start = pl.multiple_of((q * levels + l) * PITCH + LEAD, 8)
            padded[pl.ds(start, lon_cells), :] = x[l * lon_cells:(l + 1) * lon_cells]
        turned = pltpu.roll(x, 2 * q + 1, 1).reshape(cells // SUB, SUB, LANES)
        return jnp.where((pair == q)[None], turned, packed)

    packed = jnp.zeros((cells // SUB, SUB, LANES), F32)
    for c in range(CHUNKS):
        load(c).wait()
        packed = lax.fori_loop(c * per, (c + 1) * per, widen, packed, unroll=8)
    pbuf[...] = packed.reshape(cells, LANES).astype(BF16)

    pl.semaphore_wait(barrier, n_lon + n_lat - 2)

    def remote(src, dst, send, recv, device):
        return pltpu.make_async_remote_copy(
            src_ref=src, dst_ref=dst, send_sem=send, recv_sem=recv,
            device_id=device, device_id_type=MESH,
        )

    up = remote(pbuf, from_left, halo_send.at[0], halo_recv.at[0], (lon, lax.rem(lat + 1, n_lat)))
    down = remote(
        pbuf, from_right, halo_send.at[1], halo_recv.at[1], (lon, lax.rem(lat + n_lat - 1, n_lat))
    )
    pl.when(lat < n_lat - 1)(lambda: up.start())
    pl.when(lat > 0)(lambda: down.start())

    row_first[...] = padded[pl.ds(LEAD, blocks, stride=PITCH), :].astype(BF16)
    row_last[...] = padded[pl.ds(LEAD + lon_cells - 1, blocks, stride=PITCH), :].astype(BF16)
    east = remote(
        row_last, row_prev, halo_send.at[2], halo_recv.at[2], (lax.rem(lon + 1, n_lon), lat)
    )
    west = remote(
        row_first, row_next, halo_send.at[3], halo_recv.at[3], (lax.rem(lon + n_lon - 1, n_lon), lat)
    )
    east.start()
    west.start()

    pl.when(lat > 0)(lambda: up.wait_recv())
    pl.when(lat < n_lat - 1)(lambda: down.wait_recv())
    edges[...] = jnp.where(
        iota((cells, LANES), 1) % 2 == 0,
        from_left[...].astype(F32),
        pltpu.roll(from_right[...].astype(F32), LANES - 2, 1),
    )
    batch = 4
    lane = iota((batch * SUB, LANES), 1)
    first = lane == 0
    last = lane == LANES - 1
    get_coef.wait()
    along, ahead, behind = (
        jnp.concatenate([coef[i * SUB:(i + 1) * SUB, :]] * batch, axis=0) for i in range(3)
    )

    def one_group(level, group):
        step = level * groups + group
        base = pl.multiple_of(level * PITCH + group * SUB, SUB)
        edge = edges[pl.ds(pl.multiple_of(step * SUB, SUB), SUB), :]
        for t0 in range(0, TIME, batch):
            d_lon, d_lat = [], []
            for comp in range(2):
                def rows(shift):
                    parts = []
                    for t in range(t0, t0 + batch):
                        offset = (comp * TIME + t) * levels * PITCH + LEAD + shift
                        parts.append(padded[pl.ds(base + offset, SUB), :])
                    return jnp.concatenate(parts, axis=0)

                d_lon.append((rows(1) - rows(-1)) * along)
                center = rows(0)
                halo = jnp.concatenate(
                    [
                        pltpu.roll(edge, (LANES - 2 * (comp * TIME + t)) % LANES, 1)
                        for t in range(t0, t0 + batch)
                    ],
                    axis=0,
                )
                nxt = jnp.where(last, halo, pltpu.roll(center, LANES - 1, 1))
                prv = jnp.where(first, halo, pltpu.roll(center, 1, 1))
                d_lat.append(nxt * ahead - prv * behind)
            here = pl.ds(t0 * SUB, batch * SUB)
            vort_at = pl.ds(pl.multiple_of(step * LANES, LANES), LANES)
            div_at = pl.ds(pl.multiple_of((step + levels * groups) * LANES, LANES), LANES)
            x_buf[here, vort_at] = (d_lon[1] - d_lat[0]).astype(BF16)
            x_buf[here, div_at] = (d_lon[0] + d_lat[1]).astype(BF16)

    @pl.loop(0, levels)
    def _(level):
        def inner(group, carry):
            one_group(level, group)
            return carry

        lax.fori_loop(1, groups - 1, inner, 0, unroll=2)

    east.wait_recv()
    padded[pl.ds(LEAD - 1, blocks, stride=PITCH), :] = row_prev[...].astype(F32)
    west.wait_recv()
    padded[pl.ds(LEAD + lon_cells, blocks, stride=PITCH), :] = row_next[...].astype(F32)

    @pl.loop(0, levels)
    def _(level):
        def outer(end, carry):
            one_group(level, end * (groups - 1))
            return carry

        lax.fori_loop(0, 2, outer, 0, unroll=2)

    store = pltpu.make_async_copy(x_buf, x_out, out_sem)
    store.start()

    wide = 8 * LANES
    side = TIME * SUB

    def add_gram(c, carry):
        x = x_buf[:, pl.ds(pl.multiple_of(c * wide, wide), wide)]
        term = lax.dot_general(x, x, (((1,), (1,)), ((), ())), preferred_element_type=F32)
        gram[...] = gram[...] + term
        return carry

    gram[...] = jnp.zeros_like(gram)
    lax.fori_loop(0, 2 * levels * groups * LANES // wide, add_gram, 0)
    same = iota((side, side), 0) % SUB == iota((side, side), 1) % SUB
    by_time = jnp.sum(jnp.where(same, gram[...], 0.0).reshape(TIME, SUB, side), axis=1)
    fold = (iota((side, LANES), 0) // SUB == iota((side, LANES), 1)).astype(F32).astype(BF16)
    folded = dot(jnp.concatenate(split(by_time, 3), axis=0), fold)
    times = folded[:TIME] + folded[TIME:2 * TIME] + folded[2 * TIME:]
    tile = times[:SUB]
    for a in range(1, TIME // SUB):
        tile = tile + pltpu.roll(times[a * SUB:(a + 1) * SUB], a * TIME, 1)
    mine[...] = tile

    lon_copies = [
        remote(mine, lon_slots.at[d - 1], lon_send.at[d - 1], lon_recv.at[d - 1],
               (lax.rem(lon + d, n_lon), lat))
        for d in range(1, n_lon)
    ]
    for copy in lon_copies:
        copy.start()
    total = mine[...]
    for d, copy in enumerate(lon_copies):
        copy.wait_recv()
        total = total + lon_slots[d]
    band[...] = total
    lat_copies = [
        remote(band, lat_slots.at[d - 1], lat_send.at[d - 1], lat_recv.at[d - 1],
               (lon, lax.rem(lat + d, n_lat)))
        for d in range(1, n_lat)
    ]
    for copy in lat_copies:
        copy.start()
    total = band[...]
    for d, copy in enumerate(lat_copies):
        copy.wait_recv()
        total = total + lat_slots[d]

    total = total * (1.0 / rows_total)
    square = jnp.concatenate(
        [total] + [pltpu.roll(total, LANES - a * TIME, 1) for a in range(1, TIME // SUB)], axis=0
    )
    get_tables.wait()
    table3 = tables[:ALL, :].astype(BF16)
    table_aug = tables[ALL:2 * ALL, :]
    table_t = tables[2 * ALL:, :].astype(BF16)
    stacked = split(square, 3) + [jnp.zeros((TIME, LANES), BF16)]
    half = dot(table3, jnp.concatenate(stacked, axis=0))
    full = dot(jnp.concatenate(split(half, 3), axis=0), table_t)
    full = full[:ALL] + full[ALL:2 * ALL] + full[2 * ALL:]
    aug = jnp.where(iota((ALL, LANES), 1) < 64, full, table_aug)
    row = iota((COLS, LANES), 0)
    lane_a = iota((COLS, LANES), 1)
    parts = [aug[:COLS], aug[COLS:]]
    panel = 8
    for start in range(0, COLS, panel):
        columns = [
            [
                jnp.broadcast_to(parts[f][:, at:at + 1], (COLS, LANES))
                for at in range(f * COLS + start, f * COLS + start + panel)
            ]
            for f in range(FREQS)
        ]
        for j in range(panel):
            k = start + j
            for f in range(FREQS):
                cols = columns[f]
                scale = jnp.where(row > k, cols[j] * (1.0 / cols[j][k:k + 1, :]), 0.0)
                for i in range(j + 1, panel):
                    cols[i] = cols[i] - scale * cols[i][k:k + 1, :]
                parts[f] = parts[f] - scale * parts[f][k:k + 1, :]
    rows_done = []
    for f in range(FREQS):
        on_diag = lane_a == iota((COLS, LANES), 0) + f * COLS
        diag = jnp.sum(jnp.where(on_diag, parts[f], 0.0), axis=1, keepdims=True)
        rows_done.append(parts[f] / jnp.sqrt(diag))
    mix = jnp.concatenate(rows_done, axis=0)
    spread = (iota((LANES, side), 0) - 64 == iota((LANES, side), 1) // SUB).astype(F32).astype(BF16)
    wide_mix = dot(jnp.concatenate(split(mix, 2), axis=0), spread)
    tall = jnp.broadcast_to(wide_mix[:, None, :], (2 * ALL, SUB, side)).reshape(2 * ALL * SUB, side)
    keep = iota(tall.shape, 0) % SUB == iota(tall.shape, 1) % SUB
    tall = jnp.where(keep, tall, 0.0).astype(BF16)
    mix_out[:, :side] = tall[:ALL * SUB]
    mix_out[:, side:] = tall[ALL * SUB:]

    pl.when(lat < n_lat - 1)(lambda: up.wait_send())
    pl.when(lat > 0)(lambda: down.wait_send())
    for copy in [east, west] + lon_copies + lat_copies:
        copy.wait_send()
    store.wait()


def basis_kernel(mix, x, out, mix_buf, x_buf, out_buf, mix_sem, x_sem, out_sem):
    slabs, lon_cells = out.shape[1], out.shape[2]
    width = lon_cells // SUB * LANES
    pairs = lon_cells // (2 * SUB)
    get_mix = pltpu.make_async_copy(mix, mix_buf, mix_sem)
    get_mix.start()

    def get_x(i):
        part = pl.ds(pl.multiple_of(i * width, LANES), width)
        return pltpu.make_async_copy(x.at[:, part], x_buf.at[:, part], x_sem.at[i])

    def put(i, g):
        part = (slice(None), i, pl.ds(g * 2 * SUB, 2 * SUB))
        return pltpu.make_async_copy(out_buf.at[part], out.at[part], out_sem.at[i, g])

    for i in range(slabs):
        get_x(i).start()
    get_mix.wait()

    @pl.loop(0, slabs)
    def _(i):
        get_x(i).wait()
        for g in range(pairs):
            at = pl.multiple_of(i * width + g * 2 * LANES, LANES)
            part = x_buf[:, pl.ds(at, 2 * LANES)]
            res = dot(mix_buf[...], jnp.concatenate([part, part], axis=0))
            for h in range(2):
                cols = res[:, h * LANES:(h + 1) * LANES].reshape(ALL, SUB, LANES)
                out_buf[:, i, (2 * g + h) * SUB:(2 * g + h + 1) * SUB, :] = cols
            put(i, g).start()

    @pl.loop(0, slabs)
    def _(i):
        for g in range(pairs):
            put(i, g).wait()


def body(n_lon, n_lat, winds):
    _, times, levels, lon_cells, lat_cells = winds.shape
    cells = levels * lon_cells
    columns = 2 * cells // SUB * LANES
    side = TIME * SUB
    table = taper_table().astype(np.float32)
    used = n_lat * 3 * SUB + 2 * ALL + LANES
    consts = np.zeros((8192, LANES), np.float32)
    coef = lat_coefficients(n_lon * lon_cells, n_lat * lat_cells, n_lat)
    consts[:n_lat * 3 * SUB] = coef.reshape(-1, LANES)
    tables = consts[n_lat * 3 * SUB:used]
    tables[:ALL, :3 * TIME] = np.concatenate([table] * 3, axis=1)
    tables[ALL:2 * ALL, 64:64 + TIME] = table
    tables[2 * ALL:2 * ALL + TIME, :ALL] = table.T
    rows_total = 2 * levels * lon_cells * n_lon * lat_cells * n_lat
    vmem = pl.BlockSpec(memory_space=pltpu.VMEM)
    anywhere = pl.BlockSpec(memory_space=pl.ANY)
    hbm = pl.BlockSpec(memory_space=pltpu.HBM)
    blocks = 2 * TIME * levels
    dma = pltpu.SemaphoreType.DMA
    x, mix = pl.pallas_call(
        functools.partial(fields_kernel, n_lon, n_lat, levels, lon_cells, rows_total),
        out_shape=(
            jax.ShapeDtypeStruct((side, columns), BF16),
            jax.ShapeDtypeStruct((ALL * SUB, 2 * side), BF16),
        ),
        in_specs=[hbm, hbm],
        out_specs=(anywhere, vmem),
        scratch_shapes=[
            pltpu.VMEM((3 * SUB, LANES), F32),
            pltpu.VMEM((2 * ALL + LANES, LANES), F32),
            pltpu.VMEM((2 * TIME, cells, LANES), BF16),
            pltpu.VMEM((blocks * PITCH + LEAD, LANES), F32),
            pltpu.VMEM((side, columns), BF16),
            pltpu.VMEM((cells, LANES), BF16),
            pltpu.VMEM((cells, LANES), BF16),
            pltpu.VMEM((cells, LANES), BF16),
            pltpu.VMEM((cells, LANES), F32),
            pltpu.VMEM((blocks, LANES), BF16),
            pltpu.VMEM((blocks, LANES), BF16),
            pltpu.VMEM((blocks, LANES), BF16),
            pltpu.VMEM((blocks, LANES), BF16),
            pltpu.VMEM((side, side), F32),
            pltpu.VMEM((SUB, LANES), F32),
            pltpu.VMEM((n_lon - 1, SUB, LANES), F32),
            pltpu.VMEM((SUB, LANES), F32),
            pltpu.VMEM((n_lat - 1, SUB, LANES), F32),
            dma((CHUNKS,)),
            dma((2,)),
            dma(()),
            dma((4,)),
            dma((4,)),
            dma((n_lon - 1,)),
            dma((n_lon - 1,)),
            dma((n_lat - 1,)),
            dma((n_lat - 1,)),
        ],
        compiler_params=pltpu.CompilerParams(
            collective_id=0, has_side_effects=True, vmem_limit_bytes=50 * 2**20
        ),
        name="fields",
    )(
        winds.reshape(2 * TIME, cells, LANES),
        jnp.asarray(consts),
    )
    basis = pl.pallas_call(
        basis_kernel,
        out_shape=jax.ShapeDtypeStruct((ALL, 2 * levels, lon_cells, LANES), F32),
        in_specs=[anywhere, anywhere],
        out_specs=hbm,
        scratch_shapes=[
            pltpu.VMEM((ALL * SUB, 2 * side), BF16),
            pltpu.VMEM((side, columns), BF16),
            pltpu.VMEM((ALL, 2 * levels, lon_cells, LANES), F32),
            dma(()),
            dma((2 * levels,)),
            dma((2 * levels, lon_cells // (2 * SUB))),
        ],
        compiler_params=pltpu.CompilerParams(vmem_limit_bytes=20 * 2**20),
        name="basis",
    )(mix, x)
    return basis.reshape(ALL, 2, levels, lon_cells, lat_cells)


def solution(mesh):
    spec = P(None, None, None, "lon", "lat")
    run = functools.partial(body, mesh.shape["lon"], mesh.shape["lat"])
    return jax.shard_map(run, mesh=mesh, in_specs=(spec,), out_specs=spec, check_vma=False)
```

```python
import functools
import math

import jax
import jax.numpy as jnp
import ml_dtypes
import numpy as np
from jax import lax
from jax.experimental import pallas as pl
from jax.experimental.pallas import tpu as pltpu
from jax.sharding import PartitionSpec as P

TIME = 32
TAPERS = 12
FREQS = 2
COLS = 2 * TAPERS
ALL = FREQS * COLS
SUB = 8
HALF = 4
LANES = 128
PITCH = 56
LEAD = 8
CHUNKS = 4
MESH = pl.DeviceIdType.MESH
F32 = jnp.float32
BF16 = jnp.bfloat16


def taper_table():
    t = np.arange(TIME, dtype=np.float64)
    k = np.arange(TAPERS, dtype=np.float64)
    weights = math.sqrt(2.0 / (TIME + 1)) * np.sin(
        math.pi * (k[:, None] + 1.0) * (t[None, :] + 1.0) / (TIME + 1)
    )
    blocks = []
    for which in range(FREQS):
        phases = 2.0 * math.pi * (7 + 2 * which) * t / TIME
        pair = np.stack([weights * np.cos(phases), -weights * np.sin(phases)], axis=1)
        blocks.append(pair.reshape(COLS, TIME))
    return np.concatenate(blocks, axis=0).astype(np.float32).astype(ml_dtypes.bfloat16)


def lat_coefficients(grid_lon, grid_lat, bands):
    step_lon = 2.0 * math.pi / grid_lon
    step_lat = 2.6 / grid_lat
    cos_lat = np.cos(-1.3 + (np.arange(-1, grid_lat + 1) + 0.5) * step_lat)
    middle = cos_lat[1:-1]
    rows = np.stack(
        [
            1.0 / (2.0 * step_lon * middle),
            cos_lat[2:] / (2.0 * step_lat * middle),
            cos_lat[:-2] / (2.0 * step_lat * middle),
        ]
    ).astype(np.float32)
    rows = rows.reshape(3, bands, 1, LANES).transpose(1, 0, 2, 3)
    return np.broadcast_to(rows, (bands, 3, SUB, LANES)).copy()


def split(value, parts):
    pieces = []
    for _ in range(parts):
        piece = value.astype(BF16)
        pieces.append(piece)
        value = value - piece.astype(F32)
    return pieces


def iota(shape, dim):
    return lax.broadcasted_iota(jnp.int32, shape, dim)


def dot(a, b):
    return jnp.dot(a, b, preferred_element_type=F32)


def fields_kernel(
    n_lon, n_lat, levels, lon_cells, rows_total,
    winds, consts,
    x_out, mix_out,
    coef, tables, raw, padded, x_buf, pbuf, from_left, from_right, edges, row_first, row_last,
    row_prev, row_next, gram, mine, lon_slots, band, lat_slots,
    in_sem, const_sem, out_sem, halo_send, halo_recv, lon_send, lon_recv, lat_send, lat_recv,
):
    lon = lax.axis_index("lon")
    lat = lax.axis_index("lat")
    groups = lon_cells // SUB
    blocks = 2 * TIME * levels
    per = 2 * TIME // CHUNKS
    cells = levels * lon_cells

    def load(c):
        part = pl.ds(c * per, per)
        return pltpu.make_async_copy(winds.at[part], raw.at[part], in_sem.at[c])

    for c in range(CHUNKS):
        load(c).start()
    band_rows = 3 * SUB
    get_coef = pltpu.make_async_copy(
        consts.at[pl.ds(pl.multiple_of(lat * band_rows, 8), band_rows)], coef, const_sem.at[0]
    )
    get_tables = pltpu.make_async_copy(
        consts.at[pl.ds(n_lat * band_rows, tables.shape[0])], tables, const_sem.at[1]
    )
    get_coef.start()
    get_tables.start()
    from_left[...] = jnp.zeros_like(from_left)
    from_right[...] = jnp.zeros_like(from_right)

    barrier = pltpu.get_barrier_semaphore()
    for d in range(1, n_lon):
        pl.semaphore_signal(
            barrier, inc=1, device_id=(lax.rem(lon + d, n_lon), lat), device_id_type=MESH
        )
    for d in range(1, n_lat):
        pl.semaphore_signal(
            barrier, inc=1, device_id=(lon, lax.rem(lat + d, n_lat)), device_id_type=MESH
        )

    pair = iota((SUB, LANES), 1) >> 1

    def widen(q, packed):
        x = raw[q].astype(F32)
        for l in range(levels):
            start = pl.multiple_of((q * levels + l) * PITCH + LEAD, 8)
            padded[pl.ds(start, lon_cells), :] = x[l * lon_cells:(l + 1) * lon_cells]
        turned = pltpu.roll(x, 2 * q + 1, 1).reshape(cells // SUB, SUB, LANES)
        return jnp.where((pair == q)[None], turned, packed)

    packed = jnp.zeros((cells // SUB, SUB, LANES), F32)
    for c in range(CHUNKS):
        load(c).wait()
        packed = lax.fori_loop(c * per, (c + 1) * per, widen, packed, unroll=8)
    pbuf[...] = packed.reshape(cells, LANES).astype(BF16)

    pl.semaphore_wait(barrier, n_lon + n_lat - 2)

    def remote(src, dst, send, recv, device):
        return pltpu.make_async_remote_copy(
            src_ref=src, dst_ref=dst, send_sem=send, recv_sem=recv,
            device_id=device, device_id_type=MESH,
        )

    up = remote(pbuf, from_left, halo_send.at[0], halo_recv.at[0], (lon, lax.rem(lat + 1, n_lat)))
    down = remote(
        pbuf, from_right, halo_send.at[1], halo_recv.at[1], (lon, lax.rem(lat + n_lat - 1, n_lat))
    )
    pl.when(lat < n_lat - 1)(lambda: up.start())
    pl.when(lat > 0)(lambda: down.start())

    row_first[...] = padded[pl.ds(LEAD, blocks, stride=PITCH), :].astype(BF16)
    row_last[...] = padded[pl.ds(LEAD + lon_cells - 1, blocks, stride=PITCH), :].astype(BF16)
    east = remote(
        row_last, row_prev, halo_send.at[2], halo_recv.at[2], (lax.rem(lon + 1, n_lon), lat)
    )
    west = remote(
        row_first, row_next, halo_send.at[3], halo_recv.at[3], (lax.rem(lon + n_lon - 1, n_lon), lat)
    )
    east.start()
    west.start()

    pl.when(lat > 0)(lambda: up.wait_recv())
    pl.when(lat < n_lat - 1)(lambda: down.wait_recv())
    edges[...] = jnp.where(
        iota((cells, LANES), 1) % 2 == 0,
        from_left[...].astype(F32),
        pltpu.roll(from_right[...].astype(F32), LANES - 2, 1),
    )
    batch = 4
    lane = iota((batch * SUB, LANES), 1)
    first = lane == 0
    last = lane == LANES - 1
    get_coef.wait()
    along, ahead, behind = (
        jnp.concatenate([coef[i * SUB:(i + 1) * SUB, :]] * batch, axis=0) for i in range(3)
    )

    low = (iota((SUB, LANES), 0) < HALF)[None]

    def column(slab, group, h):
        pair = slab * (groups // 2) + group // 2
        at = (pair * 2 + h) * 2 + lax.rem(group, 2)
        return pl.ds(pl.multiple_of(at * LANES, LANES), LANES)

    def one_group(level, group):
        base = pl.multiple_of(level * PITCH + group * SUB, SUB)
        edge = edges[pl.ds(pl.multiple_of(level * lon_cells + group * SUB, SUB), SUB), :]
        for t0 in range(0, TIME, batch):
            d_lon, d_lat = [], []
            for comp in range(2):
                def rows(shift):
                    parts = []
                    for t in range(t0, t0 + batch):
                        offset = (comp * TIME + t) * levels * PITCH + LEAD + shift
                        parts.append(padded[pl.ds(base + offset, SUB), :])
                    return jnp.concatenate(parts, axis=0)

                d_lon.append((rows(1) - rows(-1)) * along)
                center = rows(0)
                halo = jnp.concatenate(
                    [
                        pltpu.roll(edge, (LANES - 2 * (comp * TIME + t)) % LANES, 1)
                        for t in range(t0, t0 + batch)
                    ],
                    axis=0,
                )
                nxt = jnp.where(last, halo, pltpu.roll(center, LANES - 1, 1))
                prv = jnp.where(first, halo, pltpu.roll(center, 1, 1))
                d_lat.append(nxt * ahead - prv * behind)
            for slab, field in ((0, d_lon[1] - d_lat[0]), (levels, d_lon[0] + d_lat[1])):
                by_t = field.reshape(batch // 2, 2, SUB, LANES)
                even, odd = by_t[:, 0], by_t[:, 1]
                crossed = pltpu.roll(jnp.where(low, odd, even), HALF, 1)
                halves = (jnp.where(low, even, crossed), jnp.where(low, crossed, odd))
                for h in range(2):
                    x_buf[pl.ds(t0 * HALF, batch * HALF), column(slab + level, group, h)] = (
                        halves[h].reshape(batch * HALF, LANES).astype(BF16)
                    )
        x = jnp.concatenate(
            [x_buf[:, column(slab + level, group, h)] for slab in (0, levels) for h in range(2)],
            axis=1,
        )
        gram[...] += lax.dot_general(x, x, (((1,), (1,)), ((), ())), preferred_element_type=F32)

    gram[...] = jnp.zeros_like(gram)

    @pl.loop(0, levels)
    def _(level):
        def inner(group, carry):
            one_group(level, group)
            return carry

        lax.fori_loop(1, groups - 1, inner, 0, unroll=2)

    east.wait_recv()
    padded[pl.ds(LEAD - 1, blocks, stride=PITCH), :] = row_prev[...].astype(F32)
    west.wait_recv()
    padded[pl.ds(LEAD + lon_cells, blocks, stride=PITCH), :] = row_next[...].astype(F32)

    @pl.loop(0, levels)
    def _(level):
        def outer(end, carry):
            one_group(level, end * (groups - 1))
            return carry

        lax.fori_loop(0, 2, outer, 0, unroll=2)

    store = pltpu.make_async_copy(x_buf, x_out, out_sem)
    store.start()

    side = TIME * HALF
    same = iota((side, side), 0) % HALF == iota((side, side), 1) % HALF
    fold = (iota((side, LANES), 0) // HALF == iota((side, LANES), 1)).astype(F32).astype(BF16)
    fold_t = (iota((TIME, side), 0) == iota((TIME, side), 1) // HALF).astype(F32).astype(BF16)
    masked = jnp.where(same, gram[...], 0.0)
    by_time = dot(
        jnp.concatenate([fold_t] * 3, axis=1), jnp.concatenate(split(masked, 3), axis=0)
    )
    folded = dot(jnp.concatenate(split(by_time, 3), axis=0), fold)
    times = folded[:TIME] + folded[TIME:2 * TIME] + folded[2 * TIME:]
    tile = times[:SUB]
    for a in range(1, TIME // SUB):
        tile = tile + pltpu.roll(times[a * SUB:(a + 1) * SUB], a * TIME, 1)
    mine[...] = tile

    lon_copies = [
        remote(mine, lon_slots.at[d - 1], lon_send.at[d - 1], lon_recv.at[d - 1],
               (lax.rem(lon + d, n_lon), lat))
        for d in range(1, n_lon)
    ]
    for copy in lon_copies:
        copy.start()
    total = mine[...]
    for d, copy in enumerate(lon_copies):
        copy.wait_recv()
        total = total + lon_slots[d]
    band[...] = total
    lat_copies = [
        remote(band, lat_slots.at[d - 1], lat_send.at[d - 1], lat_recv.at[d - 1],
               (lon, lax.rem(lat + d, n_lat)))
        for d in range(1, n_lat)
    ]
    for copy in lat_copies:
        copy.start()
    total = band[...]
    for d, copy in enumerate(lat_copies):
        copy.wait_recv()
        total = total + lat_slots[d]

    total = total * (1.0 / rows_total)
    square = jnp.concatenate(
        [total] + [pltpu.roll(total, LANES - a * TIME, 1) for a in range(1, TIME // SUB)], axis=0
    )
    get_tables.wait()
    table3 = tables[:ALL, :].astype(BF16)
    table_aug = tables[ALL:2 * ALL, :]
    table_t = tables[2 * ALL:, :].astype(BF16)
    stacked = split(square, 3) + [jnp.zeros((TIME, LANES), BF16)]
    half = dot(table3, jnp.concatenate(stacked, axis=0))
    full = dot(jnp.concatenate(split(half, 3), axis=0), table_t)
    full = full[:ALL] + full[ALL:2 * ALL] + full[2 * ALL:]
    aug = jnp.where(iota((ALL, LANES), 1) < 64, full, table_aug)
    row = iota((COLS, LANES), 0)
    lane_a = iota((COLS, LANES), 1)
    parts = [aug[:COLS], aug[COLS:]]
    panel = 8
    for start in range(0, COLS, panel):
        columns = [
            [
                jnp.broadcast_to(parts[f][:, at:at + 1], (COLS, LANES))
                for at in range(f * COLS + start, f * COLS + start + panel)
            ]
            for f in range(FREQS)
        ]
        for j in range(panel):
            k = start + j
            for f in range(FREQS):
                cols = columns[f]
                scale = jnp.where(row > k, cols[j] * (1.0 / cols[j][k:k + 1, :]), 0.0)
                for i in range(j + 1, panel):
                    cols[i] = cols[i] - scale * cols[i][k:k + 1, :]
                parts[f] = parts[f] - scale * parts[f][k:k + 1, :]
    rows_done = []
    for f in range(FREQS):
        on_diag = lane_a == iota((COLS, LANES), 0) + f * COLS
        diag = jnp.sum(jnp.where(on_diag, parts[f], 0.0), axis=1, keepdims=True)
        rows_done.append(parts[f] / jnp.sqrt(diag))
    mix = jnp.concatenate(rows_done, axis=0)
    spread = (iota((LANES, side), 0) - 64 == iota((LANES, side), 1) // HALF).astype(F32).astype(BF16)
    parts = dot(jnp.concatenate(split(mix, 2), axis=0), spread).astype(BF16)
    wide_mix = jnp.concatenate([parts[:ALL], parts[ALL:]], axis=1)
    tall = ALL * HALF
    r = iota((2 * tall, ALL), 0)
    source = jnp.where(r < tall, r >> 2, ((r - tall) >> 2) ^ 1)
    pick = (source == iota((2 * tall, ALL), 1)).astype(F32).astype(BF16)
    spread_rows = dot(pick, wide_mix)
    keep = iota((2 * tall, 2 * side), 0) % HALF == iota((2 * tall, 2 * side), 1) % HALF
    mix_out[...] = jnp.where(keep, spread_rows, 0.0).astype(BF16)

    pl.when(lat < n_lat - 1)(lambda: up.wait_send())
    pl.when(lat > 0)(lambda: down.wait_send())
    for copy in [east, west] + lon_copies + lat_copies:
        copy.wait_send()
    store.wait()


def basis_kernel(mix, x, out, mix_buf, x_buf, out_buf, mix_sem, x_sem, out_sem):
    slabs, lon_cells = out.shape[2], out.shape[3]
    width = lon_cells // HALF * LANES
    pairs = lon_cells // (2 * SUB)
    tall = ALL * HALF
    low = (iota((SUB, LANES), 0) < HALF)[None]
    get_mix = pltpu.make_async_copy(mix, mix_buf, mix_sem)
    get_mix.start()

    def get_x(i):
        part = pl.ds(pl.multiple_of(i * width, LANES), width)
        return pltpu.make_async_copy(x.at[:, part], x_buf.at[:, part], x_sem.at[i])

    def put(i, g):
        part = (slice(None), slice(None), i, pl.ds(g * 2 * SUB, 2 * SUB))
        return pltpu.make_async_copy(out_buf.at[part], out.at[part], out_sem.at[i, g])

    for i in range(slabs):
        get_x(i).start()
    get_mix.wait()

    @pl.loop(0, slabs)
    def _(i):
        get_x(i).wait()
        for g in range(pairs):
            res = []
            for h in range(2):
                at = pl.multiple_of(i * width + (2 * g + h) * 2 * LANES, LANES)
                part = x_buf[:, pl.ds(at, 2 * LANES)]
                rows = mix_buf[h * tall:(h + 1) * tall, :]
                res.append(dot(rows, jnp.concatenate([part, part], axis=0)))
            for w in range(2):
                near, far = (
                    r[:, w * LANES:(w + 1) * LANES].reshape(ALL // 2, SUB, LANES) for r in res
                )
                here = slice((2 * g + w) * SUB, (2 * g + w + 1) * SUB)
                out_buf[:, 0, i, here, :] = jnp.where(low, near, far)
                out_buf[:, 1, i, here, :] = pltpu.roll(jnp.where(low, far, near), HALF, 1)
            put(i, g).start()

    @pl.loop(0, slabs)
    def _(i):
        for g in range(pairs):
            put(i, g).wait()


def body(n_lon, n_lat, winds):
    _, times, levels, lon_cells, lat_cells = winds.shape
    cells = levels * lon_cells
    columns = 2 * cells // HALF * LANES
    side = TIME * HALF
    table = taper_table().astype(np.float32)
    used = n_lat * 3 * SUB + 2 * ALL + LANES
    consts = np.zeros((8192, LANES), np.float32)
    coef = lat_coefficients(n_lon * lon_cells, n_lat * lat_cells, n_lat)
    consts[:n_lat * 3 * SUB] = coef.reshape(-1, LANES)
    tables = consts[n_lat * 3 * SUB:used]
    tables[:ALL, :3 * TIME] = np.concatenate([table] * 3, axis=1)
    tables[ALL:2 * ALL, 64:64 + TIME] = table
    tables[2 * ALL:2 * ALL + TIME, :ALL] = table.T
    rows_total = 2 * levels * lon_cells * n_lon * lat_cells * n_lat
    vmem = pl.BlockSpec(memory_space=pltpu.VMEM)
    anywhere = pl.BlockSpec(memory_space=pl.ANY)
    hbm = pl.BlockSpec(memory_space=pltpu.HBM)
    blocks = 2 * TIME * levels
    dma = pltpu.SemaphoreType.DMA
    x, mix = pl.pallas_call(
        functools.partial(fields_kernel, n_lon, n_lat, levels, lon_cells, rows_total),
        out_shape=(
            jax.ShapeDtypeStruct((side, columns), BF16),
            jax.ShapeDtypeStruct((2 * ALL * HALF, 2 * side), BF16),
        ),
        in_specs=[hbm, hbm],
        out_specs=(anywhere, vmem),
        scratch_shapes=[
            pltpu.VMEM((3 * SUB, LANES), F32),
            pltpu.VMEM((2 * ALL + LANES, LANES), F32),
            pltpu.VMEM((2 * TIME, cells, LANES), BF16),
            pltpu.VMEM((blocks * PITCH + LEAD, LANES), F32),
            pltpu.VMEM((side, columns), BF16),
            pltpu.VMEM((cells, LANES), BF16),
            pltpu.VMEM((cells, LANES), BF16),
            pltpu.VMEM((cells, LANES), BF16),
            pltpu.VMEM((cells, LANES), F32),
            pltpu.VMEM((blocks, LANES), BF16),
            pltpu.VMEM((blocks, LANES), BF16),
            pltpu.VMEM((blocks, LANES), BF16),
            pltpu.VMEM((blocks, LANES), BF16),
            pltpu.VMEM((side, side), F32),
            pltpu.VMEM((SUB, LANES), F32),
            pltpu.VMEM((n_lon - 1, SUB, LANES), F32),
            pltpu.VMEM((SUB, LANES), F32),
            pltpu.VMEM((n_lat - 1, SUB, LANES), F32),
            dma((CHUNKS,)),
            dma((2,)),
            dma(()),
            dma((4,)),
            dma((4,)),
            dma((n_lon - 1,)),
            dma((n_lon - 1,)),
            dma((n_lat - 1,)),
            dma((n_lat - 1,)),
        ],
        compiler_params=pltpu.CompilerParams(
            collective_id=0, has_side_effects=True, vmem_limit_bytes=50 * 2**20
        ),
        name="fields",
    )(
        winds.reshape(2 * TIME, cells, LANES),
        jnp.asarray(consts),
    )
    basis = pl.pallas_call(
        basis_kernel,
        out_shape=jax.ShapeDtypeStruct((ALL // 2, 2, 2 * levels, lon_cells, LANES), F32),
        in_specs=[anywhere, anywhere],
        out_specs=hbm,
        scratch_shapes=[
            pltpu.VMEM((2 * ALL * HALF, 2 * side), BF16),
            pltpu.VMEM((side, columns), BF16),
            pltpu.VMEM((ALL // 2, 2, 2 * levels, lon_cells, LANES), F32),
            dma(()),
            dma((2 * levels,)),
            dma((2 * levels, lon_cells // (2 * SUB))),
        ],
        compiler_params=pltpu.CompilerParams(vmem_limit_bytes=20 * 2**20),
        name="basis",
    )(mix, x)
    return basis.reshape(ALL, 2, levels, lon_cells, lat_cells)


def solution(mesh):
    spec = P(None, None, None, "lon", "lat")
    run = functools.partial(body, mesh.shape["lon"], mesh.shape["lat"])
    return jax.shard_map(run, mesh=mesh, in_specs=(spec,), out_specs=spec, check_vma=False)
```

```python
import functools
import math

import jax
import jax.numpy as jnp
import ml_dtypes
import numpy as np
from jax import lax
from jax.experimental import pallas as pl
from jax.experimental.pallas import tpu as pltpu
from jax.sharding import PartitionSpec as P

TIME = 32
TAPERS = 12
FREQS = 2
COLS = 2 * TAPERS
ALL = FREQS * COLS
SUB = 8
HALF = 4
LANES = 128
PITCH = 56
LEAD = 8
CHUNKS = 4
MESH = pl.DeviceIdType.MESH
F32 = jnp.float32
BF16 = jnp.bfloat16


def taper_table():
    t = np.arange(TIME, dtype=np.float64)
    k = np.arange(TAPERS, dtype=np.float64)
    weights = math.sqrt(2.0 / (TIME + 1)) * np.sin(
        math.pi * (k[:, None] + 1.0) * (t[None, :] + 1.0) / (TIME + 1)
    )
    blocks = []
    for which in range(FREQS):
        phases = 2.0 * math.pi * (7 + 2 * which) * t / TIME
        pair = np.stack([weights * np.cos(phases), -weights * np.sin(phases)], axis=1)
        blocks.append(pair.reshape(COLS, TIME))
    return np.concatenate(blocks, axis=0).astype(np.float32).astype(ml_dtypes.bfloat16)


def lat_coefficients(grid_lon, grid_lat, bands):
    step_lon = 2.0 * math.pi / grid_lon
    step_lat = 2.6 / grid_lat
    cos_lat = np.cos(-1.3 + (np.arange(-1, grid_lat + 1) + 0.5) * step_lat)
    middle = cos_lat[1:-1]
    rows = np.stack(
        [
            1.0 / (2.0 * step_lon * middle),
            cos_lat[2:] / (2.0 * step_lat * middle),
            cos_lat[:-2] / (2.0 * step_lat * middle),
        ]
    ).astype(np.float32)
    rows = rows.reshape(3, bands, 1, LANES).transpose(1, 0, 2, 3)
    return np.broadcast_to(rows, (bands, 3, SUB, LANES)).copy()


def split(value, parts):
    pieces = []
    for _ in range(parts):
        piece = value.astype(BF16)
        pieces.append(piece)
        value = value - piece.astype(F32)
    return pieces


def iota(shape, dim):
    return lax.broadcasted_iota(jnp.int32, shape, dim)


def dot(a, b):
    return jnp.dot(a, b, preferred_element_type=F32)


def fields_kernel(
    n_lon, n_lat, levels, lon_cells, rows_total,
    winds, consts,
    x_out, mix_out,
    coef, tables, raw, padded, x_buf, pbuf, from_left, from_right, edges, row_first, row_last,
    row_prev, row_next, gram, mine, lon_slots, band, lat_slots,
    in_sem, const_sem, out_sem, halo_send, halo_recv, lon_send, lon_recv, lat_send, lat_recv,
):
    lon = lax.axis_index("lon")
    lat = lax.axis_index("lat")
    groups = lon_cells // SUB
    blocks = 2 * TIME * levels
    per = 2 * TIME // CHUNKS
    cells = levels * lon_cells

    def load(c):
        part = pl.ds(c * per, per)
        return pltpu.make_async_copy(winds.at[part], raw.at[part], in_sem.at[c])

    for c in range(CHUNKS):
        load(c).start()
    band_rows = 3 * SUB
    get_coef = pltpu.make_async_copy(
        consts.at[pl.ds(pl.multiple_of(lat * band_rows, 8), band_rows)], coef, const_sem.at[0]
    )
    get_tables = pltpu.make_async_copy(
        consts.at[pl.ds(n_lat * band_rows, tables.shape[0])], tables, const_sem.at[1]
    )
    get_coef.start()
    get_tables.start()
    from_left[...] = jnp.zeros_like(from_left)
    from_right[...] = jnp.zeros_like(from_right)

    barrier = pltpu.get_barrier_semaphore()
    for d in range(1, n_lon):
        pl.semaphore_signal(
            barrier, inc=1, device_id=(lax.rem(lon + d, n_lon), lat), device_id_type=MESH
        )
    for d in range(1, n_lat):
        pl.semaphore_signal(
            barrier, inc=1, device_id=(lon, lax.rem(lat + d, n_lat)), device_id_type=MESH
        )

    pair = iota((SUB, LANES), 1) >> 1

    def widen(q, packed):
        x = raw[q].astype(F32)
        for l in range(levels):
            start = pl.multiple_of((q * levels + l) * PITCH + LEAD, 8)
            padded[pl.ds(start, lon_cells), :] = x[l * lon_cells:(l + 1) * lon_cells]
        turned = pltpu.roll(x, 2 * q + 1, 1).reshape(cells // SUB, SUB, LANES)
        return jnp.where((pair == q)[None], turned, packed)

    packed = jnp.zeros((cells // SUB, SUB, LANES), F32)
    for c in range(CHUNKS):
        load(c).wait()
        packed = lax.fori_loop(c * per, (c + 1) * per, widen, packed, unroll=8)
    pbuf[...] = packed.reshape(cells, LANES).astype(BF16)

    pl.semaphore_wait(barrier, n_lon + n_lat - 2)

    def remote(src, dst, send, recv, device):
        return pltpu.make_async_remote_copy(
            src_ref=src, dst_ref=dst, send_sem=send, recv_sem=recv,
            device_id=device, device_id_type=MESH,
        )

    up = remote(pbuf, from_left, halo_send.at[0], halo_recv.at[0], (lon, lax.rem(lat + 1, n_lat)))
    down = remote(
        pbuf, from_right, halo_send.at[1], halo_recv.at[1], (lon, lax.rem(lat + n_lat - 1, n_lat))
    )
    pl.when(lat < n_lat - 1)(lambda: up.start())
    pl.when(lat > 0)(lambda: down.start())

    row_first[...] = padded[pl.ds(LEAD, blocks, stride=PITCH), :].astype(BF16)
    row_last[...] = padded[pl.ds(LEAD + lon_cells - 1, blocks, stride=PITCH), :].astype(BF16)
    east = remote(
        row_last, row_prev, halo_send.at[2], halo_recv.at[2], (lax.rem(lon + 1, n_lon), lat)
    )
    west = remote(
        row_first, row_next, halo_send.at[3], halo_recv.at[3], (lax.rem(lon + n_lon - 1, n_lon), lat)
    )
    east.start()
    west.start()

    pl.when(lat > 0)(lambda: up.wait_recv())
    pl.when(lat < n_lat - 1)(lambda: down.wait_recv())
    edges[...] = jnp.where(
        iota((cells, LANES), 1) % 2 == 0,
        from_left[...].astype(F32),
        pltpu.roll(from_right[...].astype(F32), LANES - 2, 1),
    )
    batch = 4
    lane = iota((batch * SUB, LANES), 1)
    first = lane == 0
    last = lane == LANES - 1
    get_coef.wait()
    along, ahead, behind = (
        jnp.concatenate([coef[i * SUB:(i + 1) * SUB, :]] * batch, axis=0) for i in range(3)
    )

    low = (iota((SUB, LANES), 0) < HALF)[None]

    def add_gram(which):
        x = jnp.concatenate(
            [
                x_buf[:, column(slab + level, group, h)]
                for level, group in which for slab in (0, levels) for h in range(2)
            ],
            axis=1,
        )
        gram[...] += lax.dot_general(x, x, (((1,), (1,)), ((), ())), preferred_element_type=F32)

    def column(slab, group, h):
        pair = slab * (groups // 2) + group // 2
        at = (pair * 2 + h) * 2 + group % 2
        return pl.ds(at * LANES if isinstance(at, int) else pl.multiple_of(at * LANES, LANES), LANES)

    def one_group(level, group, before):
        add_gram([(level, before)])
        base = pl.multiple_of(level * PITCH + group * SUB, SUB)
        edge = edges[pl.ds(pl.multiple_of(level * lon_cells + group * SUB, SUB), SUB), :]
        for t0 in range(0, TIME, batch):
            d_lon, d_lat = [], []
            for comp in range(2):
                def rows(shift):
                    parts = []
                    for t in range(t0, t0 + batch):
                        offset = (comp * TIME + t) * levels * PITCH + LEAD + shift
                        parts.append(padded[pl.ds(base + offset, SUB), :])
                    return jnp.concatenate(parts, axis=0)

                d_lon.append((rows(1) - rows(-1)) * along)
                center = rows(0)
                halo = jnp.concatenate(
                    [
                        pltpu.roll(edge, (LANES - 2 * (comp * TIME + t)) % LANES, 1)
                        for t in range(t0, t0 + batch)
                    ],
                    axis=0,
                )
                nxt = jnp.where(last, halo, pltpu.roll(center, LANES - 1, 1))
                prv = jnp.where(first, halo, pltpu.roll(center, 1, 1))
                d_lat.append(nxt * ahead - prv * behind)
            for slab, field in ((0, d_lon[1] - d_lat[0]), (levels, d_lon[0] + d_lat[1])):
                by_t = field.reshape(batch // 2, 2, SUB, LANES)
                even, odd = by_t[:, 0], by_t[:, 1]
                crossed = pltpu.roll(jnp.where(low, odd, even), HALF, 1)
                halves = (jnp.where(low, even, crossed), jnp.where(low, crossed, odd))
                for h in range(2):
                    x_buf[pl.ds(t0 * HALF, batch * HALF), column(slab + level, group, h)] = (
                        halves[h].reshape(batch * HALF, LANES).astype(BF16)
                    )
    gram[...] = jnp.zeros_like(gram)
    for slab in range(2 * levels):
        for h in range(2):
            x_buf[:, column(slab, 0, h)] = jnp.zeros((TIME * HALF, LANES), BF16)

    @pl.loop(0, levels)
    def _(level):
        def inner(group, carry):
            one_group(level, group, group - 1)
            return carry

        lax.fori_loop(1, groups - 1, inner, 0, unroll=2)

    east.wait_recv()
    padded[pl.ds(LEAD - 1, blocks, stride=PITCH), :] = row_prev[...].astype(F32)
    west.wait_recv()
    padded[pl.ds(LEAD + lon_cells, blocks, stride=PITCH), :] = row_next[...].astype(F32)

    @pl.loop(0, levels)
    def _(level):
        def outer(end, carry):
            one_group(level, end * (groups - 1), (1 - end) * (groups - 2))
            return carry

        lax.fori_loop(0, 2, outer, 0, unroll=2)

    add_gram([(level, groups - 1) for level in range(levels)])
    store = pltpu.make_async_copy(x_buf, x_out, out_sem)
    store.start()

    side = TIME * HALF
    same = iota((side, side), 0) % HALF == iota((side, side), 1) % HALF
    fold = (iota((side, LANES), 0) // HALF == iota((side, LANES), 1)).astype(F32).astype(BF16)
    fold_t = (iota((TIME, side), 0) == iota((TIME, side), 1) // HALF).astype(F32).astype(BF16)
    masked = jnp.where(same, gram[...], 0.0)
    by_time = dot(
        jnp.concatenate([fold_t] * 3, axis=1), jnp.concatenate(split(masked, 3), axis=0)
    )
    folded = dot(jnp.concatenate(split(by_time, 3), axis=0), fold)
    times = folded[:TIME] + folded[TIME:2 * TIME] + folded[2 * TIME:]
    tile = times[:SUB]
    for a in range(1, TIME // SUB):
        tile = tile + pltpu.roll(times[a * SUB:(a + 1) * SUB], a * TIME, 1)
    mine[...] = tile

    lon_copies = [
        remote(mine, lon_slots.at[d - 1], lon_send.at[d - 1], lon_recv.at[d - 1],
               (lax.rem(lon + d, n_lon), lat))
        for d in range(1, n_lon)
    ]
    for copy in lon_copies:
        copy.start()
    get_tables.wait()
    table3 = tables[:ALL, :].astype(BF16)
    table_aug = tables[ALL:2 * ALL, :]
    table_t = tables[2 * ALL:, :].astype(BF16)
    spread = (iota((LANES, side), 0) - 64 == iota((LANES, side), 1) // HALF).astype(F32).astype(BF16)
    tall = ALL * HALF
    r = iota((2 * tall, ALL), 0)
    source = jnp.where(r < tall, r >> 2, ((r - tall) >> 2) ^ 1)
    pick = (source == iota((2 * tall, ALL), 1)).astype(F32).astype(BF16)
    total = mine[...]
    for d, copy in enumerate(lon_copies):
        copy.wait_recv()
        total = total + lon_slots[d]
    band[...] = total
    lat_copies = [
        remote(band, lat_slots.at[d - 1], lat_send.at[d - 1], lat_recv.at[d - 1],
               (lon, lax.rem(lat + d, n_lat)))
        for d in range(1, n_lat)
    ]
    for copy in lat_copies:
        copy.start()
    total = band[...]
    for d, copy in enumerate(lat_copies):
        copy.wait_recv()
        total = total + lat_slots[d]

    total = total * (1.0 / rows_total)
    square = jnp.concatenate(
        [total] + [pltpu.roll(total, LANES - a * TIME, 1) for a in range(1, TIME // SUB)], axis=0
    )
    stacked = split(square, 3) + [jnp.zeros((TIME, LANES), BF16)]
    half = dot(table3, jnp.concatenate(stacked, axis=0))
    full = dot(jnp.concatenate(split(half, 3), axis=0), table_t)
    full = full[:ALL] + full[ALL:2 * ALL] + full[2 * ALL:]
    aug = jnp.where(iota((ALL, LANES), 1) < 64, full, table_aug)
    row = iota((COLS, LANES), 0)
    lane_a = iota((COLS, LANES), 1)
    parts = [aug[:COLS], aug[COLS:]]
    panel = 8
    for start in range(0, COLS, panel):
        columns = [
            [
                jnp.broadcast_to(parts[f][:, at:at + 1], (COLS, LANES))
                for at in range(f * COLS + start, f * COLS + start + panel)
            ]
            for f in range(FREQS)
        ]
        for j in range(panel):
            k = start + j
            for f in range(FREQS):
                cols = columns[f]
                scale = jnp.where(row > k, cols[j] * (1.0 / cols[j][k:k + 1, :]), 0.0)
                for i in range(j + 1, panel):
                    cols[i] = cols[i] - scale * cols[i][k:k + 1, :]
                parts[f] = parts[f] - scale * parts[f][k:k + 1, :]
    rows_done = []
    for f in range(FREQS):
        on_diag = lane_a == iota((COLS, LANES), 0) + f * COLS
        diag = jnp.sum(jnp.where(on_diag, parts[f], 0.0), axis=1, keepdims=True)
        rows_done.append(parts[f] / jnp.sqrt(diag))
    mix = jnp.concatenate(rows_done, axis=0)
    parts = dot(jnp.concatenate(split(mix, 2), axis=0), spread).astype(BF16)
    wide_mix = jnp.concatenate([parts[:ALL], parts[ALL:]], axis=1)
    spread_rows = dot(pick, wide_mix)
    keep = (iota((2 * tall, 2 * side), 0) & 3) == (iota((2 * tall, 2 * side), 1) & 3)
    mix_out[...] = jnp.where(keep, spread_rows, 0.0).astype(BF16)

    pl.when(lat < n_lat - 1)(lambda: up.wait_send())
    pl.when(lat > 0)(lambda: down.wait_send())
    for copy in [east, west] + lon_copies + lat_copies:
        copy.wait_send()
    store.wait()


def basis_kernel(mix_buf, x_buf, out, out_buf, out_sem):
    slabs, lon_cells = out.shape[2], out.shape[3]
    width = lon_cells // HALF * LANES
    pairs = lon_cells // (2 * SUB)
    tall = ALL * HALF
    low = (iota((SUB, LANES), 0) < HALF)[None]

    def put(i, g):
        part = (slice(None), slice(None), i, pl.ds(g * 2 * SUB, 2 * SUB))
        return pltpu.make_async_copy(out_buf.at[part], out.at[part], out_sem.at[i, g])

    @pl.loop(0, slabs)
    def _(i):
        for g in range(pairs):
            res = []
            for h in range(2):
                at = pl.multiple_of(i * width + (2 * g + h) * 2 * LANES, LANES)
                part = x_buf[:, pl.ds(at, 2 * LANES)]
                rows = mix_buf[h * tall:(h + 1) * tall, :]
                res.append(dot(rows, jnp.concatenate([part, part], axis=0)))
            for w in range(2):
                near, far = (
                    r[:, w * LANES:(w + 1) * LANES].reshape(ALL // 2, SUB, LANES) for r in res
                )
                here = slice((2 * g + w) * SUB, (2 * g + w + 1) * SUB)
                out_buf[:, 0, i, here, :] = jnp.where(low, near, far)
                out_buf[:, 1, i, here, :] = pltpu.roll(jnp.where(low, far, near), HALF, 1)
            put(i, g).start()

    @pl.loop(0, slabs)
    def _(i):
        for g in range(pairs):
            put(i, g).wait()


def body(n_lon, n_lat, winds):
    _, times, levels, lon_cells, lat_cells = winds.shape
    cells = levels * lon_cells
    columns = 2 * cells // HALF * LANES
    side = TIME * HALF
    table = taper_table().astype(np.float32)
    used = n_lat * 3 * SUB + 2 * ALL + LANES
    consts = np.zeros((8192, LANES), np.float32)
    coef = lat_coefficients(n_lon * lon_cells, n_lat * lat_cells, n_lat)
    consts[:n_lat * 3 * SUB] = coef.reshape(-1, LANES)
    tables = consts[n_lat * 3 * SUB:used]
    tables[:ALL, :3 * TIME] = np.concatenate([table] * 3, axis=1)
    tables[ALL:2 * ALL, 64:64 + TIME] = table
    tables[2 * ALL:2 * ALL + TIME, :ALL] = table.T
    rows_total = 2 * levels * lon_cells * n_lon * lat_cells * n_lat
    vmem = pl.BlockSpec(memory_space=pltpu.VMEM)
    anywhere = pl.BlockSpec(memory_space=pl.ANY)
    hbm = pl.BlockSpec(memory_space=pltpu.HBM)
    blocks = 2 * TIME * levels
    dma = pltpu.SemaphoreType.DMA
    x, mix = pl.pallas_call(
        functools.partial(fields_kernel, n_lon, n_lat, levels, lon_cells, rows_total),
        out_shape=(
            jax.ShapeDtypeStruct((side, columns), BF16),
            jax.ShapeDtypeStruct((2 * ALL * HALF, 2 * side), BF16),
        ),
        in_specs=[hbm, hbm],
        out_specs=(anywhere, vmem),
        scratch_shapes=[
            pltpu.VMEM((3 * SUB, LANES), F32),
            pltpu.VMEM((2 * ALL + LANES, LANES), F32),
            pltpu.VMEM((2 * TIME, cells, LANES), BF16),
            pltpu.VMEM((blocks * PITCH + LEAD, LANES), F32),
            pltpu.VMEM((side, columns), BF16),
            pltpu.VMEM((cells, LANES), BF16),
            pltpu.VMEM((cells, LANES), BF16),
            pltpu.VMEM((cells, LANES), BF16),
            pltpu.VMEM((cells, LANES), F32),
            pltpu.VMEM((blocks, LANES), BF16),
            pltpu.VMEM((blocks, LANES), BF16),
            pltpu.VMEM((blocks, LANES), BF16),
            pltpu.VMEM((blocks, LANES), BF16),
            pltpu.VMEM((side, side), F32),
            pltpu.VMEM((SUB, LANES), F32),
            pltpu.VMEM((n_lon - 1, SUB, LANES), F32),
            pltpu.VMEM((SUB, LANES), F32),
            pltpu.VMEM((n_lat - 1, SUB, LANES), F32),
            dma((CHUNKS,)),
            dma((2,)),
            dma(()),
            dma((4,)),
            dma((4,)),
            dma((n_lon - 1,)),
            dma((n_lon - 1,)),
            dma((n_lat - 1,)),
            dma((n_lat - 1,)),
        ],
        compiler_params=pltpu.CompilerParams(
            collective_id=0, has_side_effects=True, vmem_limit_bytes=50 * 2**20
        ),
        name="fields",
    )(
        winds.reshape(2 * TIME, cells, LANES),
        jnp.asarray(consts),
    )
    basis = pl.pallas_call(
        basis_kernel,
        out_shape=jax.ShapeDtypeStruct((ALL // 2, 2, 2 * levels, lon_cells, LANES), F32),
        in_specs=[vmem, vmem],
        out_specs=hbm,
        scratch_shapes=[
            pltpu.VMEM((ALL // 2, 2, 2 * levels, lon_cells, LANES), F32),
            dma((2 * levels, lon_cells // (2 * SUB))),
        ],
        compiler_params=pltpu.CompilerParams(vmem_limit_bytes=20 * 2**20),
        name="basis",
    )(mix, x)
    return basis.reshape(ALL, 2, levels, lon_cells, lat_cells)


def solution(mesh):
    spec = P(None, None, None, "lon", "lat")
    run = functools.partial(body, mesh.shape["lon"], mesh.shape["lat"])
    return jax.shard_map(run, mesh=mesh, in_specs=(spec,), out_specs=spec, check_vma=False)
```

```python
import functools
import math

import jax
import jax.numpy as jnp
import ml_dtypes
import numpy as np
from jax import lax
from jax.experimental import pallas as pl
from jax.experimental.pallas import tpu as pltpu
from jax.sharding import PartitionSpec as P

TIME = 32
TAPERS = 12
FREQS = 2
COLS = 2 * TAPERS
ALL = FREQS * COLS
SUB = 8
HALF = 4
LANES = 128
PITCH = 56
LEAD = 8
CHUNKS = 4
BATCH = 4
MESH = pl.DeviceIdType.MESH
F32 = jnp.float32
BF16 = jnp.bfloat16


def taper_table():
    t = np.arange(TIME, dtype=np.float64)
    k = np.arange(TAPERS, dtype=np.float64)
    weights = math.sqrt(2.0 / (TIME + 1)) * np.sin(
        math.pi * (k[:, None] + 1.0) * (t[None, :] + 1.0) / (TIME + 1)
    )
    blocks = []
    for which in range(FREQS):
        phases = 2.0 * math.pi * (7 + 2 * which) * t / TIME
        pair = np.stack([weights * np.cos(phases), -weights * np.sin(phases)], axis=1)
        blocks.append(pair.reshape(COLS, TIME))
    return np.concatenate(blocks, axis=0).astype(np.float32).astype(ml_dtypes.bfloat16)


def lat_coefficients(grid_lon, grid_lat, bands):
    step_lon = 2.0 * math.pi / grid_lon
    step_lat = 2.6 / grid_lat
    cos_lat = np.cos(-1.3 + (np.arange(-1, grid_lat + 1) + 0.5) * step_lat)
    middle = cos_lat[1:-1]
    rows = np.stack(
        [
            1.0 / (2.0 * step_lon * middle),
            cos_lat[2:] / (2.0 * step_lat * middle),
            cos_lat[:-2] / (2.0 * step_lat * middle),
        ]
    ).astype(np.float32)
    rows = rows.reshape(3, bands, 1, LANES).transpose(1, 0, 2, 3)
    return np.broadcast_to(rows, (bands, 3, SUB, LANES)).copy()


def split(value, parts):
    pieces = []
    for _ in range(parts):
        piece = value.astype(BF16)
        pieces.append(piece)
        value = value - piece.astype(F32)
    return pieces


def iota(shape, dim):
    return lax.broadcasted_iota(jnp.int32, shape, dim)


def dot(a, b):
    return jnp.dot(a, b, preferred_element_type=F32)


def fields_kernel(
    n_lon, n_lat, levels, lon_cells, rows_total,
    winds, consts,
    x_out, mix_out,
    coef, tables, raw, padded, x_buf, pbuf, from_left, from_right, edges, row_first, row_last,
    row_prev, row_next, kept, gram, mine, lon_slots, band, lat_slots,
    in_sem, const_sem, out_sem, halo_send, halo_recv, lon_send, lon_recv, lat_send, lat_recv,
):
    lon = lax.axis_index("lon")
    lat = lax.axis_index("lat")
    groups = lon_cells // SUB
    blocks = 2 * TIME * levels
    per = 2 * TIME // CHUNKS
    cells = levels * lon_cells

    def load(c):
        part = pl.ds(c * per, per)
        return pltpu.make_async_copy(winds.at[part], raw.at[part], in_sem.at[c])

    for c in range(CHUNKS):
        load(c).start()
    band_rows = 3 * SUB
    get_coef = pltpu.make_async_copy(
        consts.at[pl.ds(pl.multiple_of(lat * band_rows, 8), band_rows)], coef, const_sem.at[0]
    )
    get_tables = pltpu.make_async_copy(
        consts.at[pl.ds(n_lat * band_rows, tables.shape[0])], tables, const_sem.at[1]
    )
    get_coef.start()
    get_tables.start()
    from_left[...] = jnp.zeros_like(from_left)
    from_right[...] = jnp.zeros_like(from_right)

    barrier = pltpu.get_barrier_semaphore()
    for d in range(1, n_lon):
        pl.semaphore_signal(
            barrier, inc=1, device_id=(lax.rem(lon + d, n_lon), lat), device_id_type=MESH
        )
    for d in range(1, n_lat):
        pl.semaphore_signal(
            barrier, inc=1, device_id=(lon, lax.rem(lat + d, n_lat)), device_id_type=MESH
        )

    pair = iota((SUB, LANES), 1) >> 1

    def widen(q, packed):
        x = raw[q].astype(F32)
        for l in range(levels):
            start = pl.multiple_of((q * levels + l) * PITCH + LEAD, 8)
            padded[pl.ds(start, lon_cells), :] = x[l * lon_cells:(l + 1) * lon_cells]
        turned = pltpu.roll(x, 2 * q + 1, 1).reshape(cells // SUB, SUB, LANES)
        return jnp.where((pair == q)[None], turned, packed)

    packed = jnp.zeros((cells // SUB, SUB, LANES), F32)
    for c in range(CHUNKS):
        load(c).wait()
        packed = lax.fori_loop(c * per, (c + 1) * per, widen, packed, unroll=8)
    pbuf[...] = packed.reshape(cells, LANES).astype(BF16)

    pl.semaphore_wait(barrier, n_lon + n_lat - 2)

    def remote(src, dst, send, recv, device):
        return pltpu.make_async_remote_copy(
            src_ref=src, dst_ref=dst, send_sem=send, recv_sem=recv,
            device_id=device, device_id_type=MESH,
        )

    up = remote(pbuf, from_left, halo_send.at[0], halo_recv.at[0], (lon, lax.rem(lat + 1, n_lat)))
    down = remote(
        pbuf, from_right, halo_send.at[1], halo_recv.at[1], (lon, lax.rem(lat + n_lat - 1, n_lat))
    )
    pl.when(lat < n_lat - 1)(lambda: up.start())
    pl.when(lat > 0)(lambda: down.start())

    row_first[...] = padded[pl.ds(LEAD, blocks, stride=PITCH), :].astype(BF16)
    row_last[...] = padded[pl.ds(LEAD + lon_cells - 1, blocks, stride=PITCH), :].astype(BF16)
    east = remote(
        row_last, row_prev, halo_send.at[2], halo_recv.at[2], (lax.rem(lon + 1, n_lon), lat)
    )
    west = remote(
        row_first, row_next, halo_send.at[3], halo_recv.at[3], (lax.rem(lon + n_lon - 1, n_lon), lat)
    )
    east.start()
    west.start()

    batch = BATCH
    lane = iota((batch * SUB, LANES), 1)
    first = lane == 0
    last = lane == LANES - 1
    get_coef.wait()
    along, ahead, behind = (
        jnp.concatenate([coef[i * SUB:(i + 1) * SUB, :]] * batch, axis=0) for i in range(3)
    )
    ahead_in = jnp.where(last, 0.0, ahead)
    behind_in = jnp.where(first, 0.0, behind)
    edge_factor = jnp.where(last, ahead, jnp.where(first, -behind, 0.0))

    low = (iota((SUB, LANES), 0) < HALF)[None]

    def add_gram(which):
        x = jnp.concatenate(
            [
                x_buf[:, column(slab + level, group, h)]
                for level, group in which for slab in (0, levels) for h in range(2)
            ],
            axis=1,
        )
        gram[...] += lax.dot_general(x, x, (((1,), (1,)), ((), ())), preferred_element_type=F32)

    def column(slab, group, h):
        pair = slab * (groups // 2) + group // 2
        at = (pair * 2 + h) * 2 + group % 2
        return pl.ds(at * LANES if isinstance(at, int) else pl.multiple_of(at * LANES, LANES), LANES)

    def without_halo(level, group, t0):
        base = pl.multiple_of(level * PITCH + group * SUB, SUB)
        d_lon, d_lat = [], []
        for comp in range(2):
            def rows(shift):
                parts = []
                for t in range(t0, t0 + batch):
                    offset = (comp * TIME + t) * levels * PITCH + LEAD + shift
                    parts.append(padded[pl.ds(base + offset, SUB), :])
                return jnp.concatenate(parts, axis=0)

            d_lon.append((rows(1) - rows(-1)) * along)
            center = rows(0)
            d_lat.append(
                pltpu.roll(center, LANES - 1, 1) * ahead_in - pltpu.roll(center, 1, 1) * behind_in
            )
        return d_lon[1] - d_lat[0], d_lon[0] + d_lat[1]

    def one_group(level, group, before, begun):
        add_gram([(level, before)])
        edge = edges[pl.ds(pl.multiple_of(level * lon_cells + group * SUB, SUB), SUB), :]
        for t0 in range(0, TIME, batch):
            halo = [
                edge_factor * jnp.concatenate(
                    [
                        pltpu.roll(edge, (LANES - 2 * (comp * TIME + t)) % LANES, 1)
                        for t in range(t0, t0 + batch)
                    ],
                    axis=0,
                )
                for comp in range(2)
            ]
            if begun:
                vort, div = (kept[f, t0 // batch, level, group] for f in range(2))
            else:
                vort, div = without_halo(level, group, t0)
            for slab, field in ((0, vort - halo[0]), (levels, div + halo[1])):
                by_t = field.reshape(batch // 2, 2, SUB, LANES)
                even, odd = by_t[:, 0], by_t[:, 1]
                crossed = pltpu.roll(jnp.where(low, odd, even), HALF, 1)
                halves = (jnp.where(low, even, crossed), jnp.where(low, crossed, odd))
                for h in range(2):
                    x_buf[pl.ds(t0 * HALF, batch * HALF), column(slab + level, group, h)] = (
                        halves[h].reshape(batch * HALF, LANES).astype(BF16)
                    )
    @pl.loop(0, levels)
    def _(level):
        def early(group, carry):
            for t0 in range(0, TIME, batch):
                vort, div = without_halo(level, group, t0)
                kept[0, t0 // batch, level, group] = vort
                kept[1, t0 // batch, level, group] = div
            return carry

        lax.fori_loop(1, groups - 1, early, 0, unroll=2)

    pl.when(lat > 0)(lambda: up.wait_recv())
    pl.when(lat < n_lat - 1)(lambda: down.wait_recv())
    edges[...] = jnp.where(
        iota((cells, LANES), 1) % 2 == 0,
        from_left[...].astype(F32),
        pltpu.roll(from_right[...].astype(F32), LANES - 2, 1),
    )
    gram[...] = jnp.zeros_like(gram)
    for slab in range(2 * levels):
        for h in range(2):
            x_buf[:, column(slab, 0, h)] = jnp.zeros((TIME * HALF, LANES), BF16)

    @pl.loop(0, levels)
    def _(level):
        def inner(group, carry):
            one_group(level, group, group - 1, True)
            return carry

        lax.fori_loop(1, groups - 1, inner, 0, unroll=2)

    east.wait_recv()
    padded[pl.ds(LEAD - 1, blocks, stride=PITCH), :] = row_prev[...].astype(F32)
    west.wait_recv()
    padded[pl.ds(LEAD + lon_cells, blocks, stride=PITCH), :] = row_next[...].astype(F32)

    @pl.loop(0, levels)
    def _(level):
        def outer(end, carry):
            one_group(level, end * (groups - 1), (1 - end) * (groups - 2), False)
            return carry

        lax.fori_loop(0, 2, outer, 0, unroll=2)

    add_gram([(level, groups - 1) for level in range(levels)])
    store = pltpu.make_async_copy(x_buf, x_out, out_sem)
    store.start()

    side = TIME * HALF
    same = iota((side, side), 0) % HALF == iota((side, side), 1) % HALF
    fold = (iota((side, LANES), 0) // HALF == iota((side, LANES), 1)).astype(F32).astype(BF16)
    fold_t = (iota((TIME, side), 0) == iota((TIME, side), 1) // HALF).astype(F32).astype(BF16)
    masked = jnp.where(same, gram[...], 0.0)
    by_time = dot(
        jnp.concatenate([fold_t] * 3, axis=1), jnp.concatenate(split(masked, 3), axis=0)
    )
    folded = dot(jnp.concatenate(split(by_time, 3), axis=0), fold)
    times = folded[:TIME] + folded[TIME:2 * TIME] + folded[2 * TIME:]
    tile = times[:SUB]
    for a in range(1, TIME // SUB):
        tile = tile + pltpu.roll(times[a * SUB:(a + 1) * SUB], a * TIME, 1)
    mine[...] = tile

    lon_copies = [
        remote(mine, lon_slots.at[d - 1], lon_send.at[d - 1], lon_recv.at[d - 1],
               (lax.rem(lon + d, n_lon), lat))
        for d in range(1, n_lon)
    ]
    for copy in lon_copies:
        copy.start()
    get_tables.wait()
    table3 = tables[:ALL, :].astype(BF16)
    table_aug = tables[ALL:2 * ALL, :]
    table_t = tables[2 * ALL:, :].astype(BF16)
    spread = (iota((LANES, side), 0) - 64 == iota((LANES, side), 1) // HALF).astype(F32).astype(BF16)
    tall = ALL * HALF
    r = iota((2 * tall, ALL), 0)
    source = jnp.where(r < tall, r >> 2, ((r - tall) >> 2) ^ 1)
    pick = (source == iota((2 * tall, ALL), 1)).astype(F32).astype(BF16)
    total = mine[...]
    for d, copy in enumerate(lon_copies):
        copy.wait_recv()
        total = total + lon_slots[d]
    band[...] = total
    lat_copies = [
        remote(band, lat_slots.at[d - 1], lat_send.at[d - 1], lat_recv.at[d - 1],
               (lon, lax.rem(lat + d, n_lat)))
        for d in range(1, n_lat)
    ]
    for copy in lat_copies:
        copy.start()
    total = band[...]
    for d, copy in enumerate(lat_copies):
        copy.wait_recv()
        total = total + lat_slots[d]

    total = total * (1.0 / rows_total)
    square = jnp.concatenate(
        [total] + [pltpu.roll(total, LANES - a * TIME, 1) for a in range(1, TIME // SUB)], axis=0
    )
    stacked = split(square, 3) + [jnp.zeros((TIME, LANES), BF16)]
    half = dot(table3, jnp.concatenate(stacked, axis=0))
    full = dot(jnp.concatenate(split(half, 3), axis=0), table_t)
    full = full[:ALL] + full[ALL:2 * ALL] + full[2 * ALL:]
    aug = jnp.where(iota((ALL, LANES), 1) < 64, full, table_aug)
    row = iota((COLS, LANES), 0)
    lane_a = iota((COLS, LANES), 1)
    parts = [aug[:COLS], aug[COLS:]]
    panel = 8
    for start in range(0, COLS, panel):
        columns = [
            [
                jnp.broadcast_to(parts[f][:, at:at + 1], (COLS, LANES))
                for at in range(f * COLS + start, f * COLS + start + panel)
            ]
            for f in range(FREQS)
        ]
        for j in range(panel):
            k = start + j
            for f in range(FREQS):
                cols = columns[f]
                pivot = cols[j][k:k + 1, :]
                guess = pl.reciprocal(pivot, approx=True)
                inverse = guess * (2.0 - pivot * guess)
                scale = jnp.where(row > k, cols[j] * inverse, 0.0)
                for i in range(j + 1, panel):
                    cols[i] = cols[i] - scale * cols[i][k:k + 1, :]
                parts[f] = parts[f] - scale * parts[f][k:k + 1, :]
    rows_done = []
    for f in range(FREQS):
        on_diag = lane_a == iota((COLS, LANES), 0) + f * COLS
        diag = jnp.sum(jnp.where(on_diag, parts[f], 0.0), axis=1, keepdims=True)
        rows_done.append(parts[f] / jnp.sqrt(diag))
    mix = jnp.concatenate(rows_done, axis=0)
    parts = dot(jnp.concatenate(split(mix, 2), axis=0), spread).astype(BF16)
    wide_mix = jnp.concatenate([parts[:ALL], parts[ALL:]], axis=1)
    spread_rows = dot(pick, wide_mix)
    keep = (iota((2 * tall, 2 * side), 0) & 3) == (iota((2 * tall, 2 * side), 1) & 3)
    mix_out[...] = jnp.where(keep, spread_rows, 0.0).astype(BF16)

    pl.when(lat < n_lat - 1)(lambda: up.wait_send())
    pl.when(lat > 0)(lambda: down.wait_send())
    for copy in [east, west] + lon_copies + lat_copies:
        copy.wait_send()
    store.wait()


def basis_kernel(mix_buf, x_buf, out, out_buf, out_sem):
    slabs, lon_cells = out.shape[2], out.shape[3]
    width = lon_cells // HALF * LANES
    pairs = lon_cells // (2 * SUB)
    tall = ALL * HALF
    low = (iota((SUB, LANES), 0) < HALF)[None]

    def put(i, g):
        part = (slice(None), slice(None), i, pl.ds(g * 2 * SUB, 2 * SUB))
        return pltpu.make_async_copy(out_buf.at[part], out.at[part], out_sem.at[i, g])

    @pl.loop(0, slabs)
    def _(i):
        for g in range(pairs):
            res = []
            for h in range(2):
                at = pl.multiple_of(i * width + (2 * g + h) * 2 * LANES, LANES)
                part = x_buf[:, pl.ds(at, 2 * LANES)]
                rows = mix_buf[h * tall:(h + 1) * tall, :]
                res.append(dot(rows, jnp.concatenate([part, part], axis=0)))
            for w in range(2):
                near, far = (
                    r[:, w * LANES:(w + 1) * LANES].reshape(ALL // 2, SUB, LANES) for r in res
                )
                here = slice((2 * g + w) * SUB, (2 * g + w + 1) * SUB)
                out_buf[:, 0, i, here, :] = jnp.where(low, near, far)
                out_buf[:, 1, i, here, :] = pltpu.roll(jnp.where(low, far, near), HALF, 1)
            put(i, g).start()

    @pl.loop(0, slabs)
    def _(i):
        for g in range(pairs):
            put(i, g).wait()


def body(n_lon, n_lat, winds):
    _, times, levels, lon_cells, lat_cells = winds.shape
    cells = levels * lon_cells
    columns = 2 * cells // HALF * LANES
    side = TIME * HALF
    table = taper_table().astype(np.float32)
    used = n_lat * 3 * SUB + 2 * ALL + LANES
    consts = np.zeros((8192, LANES), np.float32)
    coef = lat_coefficients(n_lon * lon_cells, n_lat * lat_cells, n_lat)
    consts[:n_lat * 3 * SUB] = coef.reshape(-1, LANES)
    tables = consts[n_lat * 3 * SUB:used]
    tables[:ALL, :3 * TIME] = np.concatenate([table] * 3, axis=1)
    tables[ALL:2 * ALL, 64:64 + TIME] = table
    tables[2 * ALL:2 * ALL + TIME, :ALL] = table.T
    rows_total = 2 * levels * lon_cells * n_lon * lat_cells * n_lat
    vmem = pl.BlockSpec(memory_space=pltpu.VMEM)
    anywhere = pl.BlockSpec(memory_space=pl.ANY)
    hbm = pl.BlockSpec(memory_space=pltpu.HBM)
    blocks = 2 * TIME * levels
    dma = pltpu.SemaphoreType.DMA
    x, mix = pl.pallas_call(
        functools.partial(fields_kernel, n_lon, n_lat, levels, lon_cells, rows_total),
        out_shape=(
            jax.ShapeDtypeStruct((side, columns), BF16),
            jax.ShapeDtypeStruct((2 * ALL * HALF, 2 * side), BF16),
        ),
        in_specs=[hbm, hbm],
        out_specs=(anywhere, vmem),
        scratch_shapes=[
            pltpu.VMEM((3 * SUB, LANES), F32),
            pltpu.VMEM((2 * ALL + LANES, LANES), F32),
            pltpu.VMEM((2 * TIME, cells, LANES), BF16),
            pltpu.VMEM((blocks * PITCH + LEAD, LANES), F32),
            pltpu.VMEM((side, columns), BF16),
            pltpu.VMEM((cells, LANES), BF16),
            pltpu.VMEM((cells, LANES), BF16),
            pltpu.VMEM((cells, LANES), BF16),
            pltpu.VMEM((cells, LANES), F32),
            pltpu.VMEM((blocks, LANES), BF16),
            pltpu.VMEM((blocks, LANES), BF16),
            pltpu.VMEM((blocks, LANES), BF16),
            pltpu.VMEM((blocks, LANES), BF16),
            pltpu.VMEM((2, TIME // BATCH, levels, lon_cells // SUB, BATCH * SUB, LANES), F32),
            pltpu.VMEM((side, side), F32),
            pltpu.VMEM((SUB, LANES), F32),
            pltpu.VMEM((n_lon - 1, SUB, LANES), F32),
            pltpu.VMEM((SUB, LANES), F32),
            pltpu.VMEM((n_lat - 1, SUB, LANES), F32),
            dma((CHUNKS,)),
            dma((2,)),
            dma(()),
            dma((4,)),
            dma((4,)),
            dma((n_lon - 1,)),
            dma((n_lon - 1,)),
            dma((n_lat - 1,)),
            dma((n_lat - 1,)),
        ],
        compiler_params=pltpu.CompilerParams(
            collective_id=0, has_side_effects=True, vmem_limit_bytes=50 * 2**20
        ),
        name="fields",
    )(
        winds.reshape(2 * TIME, cells, LANES),
        jnp.asarray(consts),
    )
    basis = pl.pallas_call(
        basis_kernel,
        out_shape=jax.ShapeDtypeStruct((ALL // 2, 2, 2 * levels, lon_cells, LANES), F32),
        in_specs=[vmem, vmem],
        out_specs=hbm,
        scratch_shapes=[
            pltpu.VMEM((ALL // 2, 2, 2 * levels, lon_cells, LANES), F32),
            dma((2 * levels, lon_cells // (2 * SUB))),
        ],
        compiler_params=pltpu.CompilerParams(vmem_limit_bytes=20 * 2**20),
        name="basis",
    )(mix, x)
    return basis.reshape(ALL, 2, levels, lon_cells, lat_cells)


def solution(mesh):
    spec = P(None, None, None, "lon", "lat")
    run = functools.partial(body, mesh.shape["lon"], mesh.shape["lat"])
    return jax.shard_map(run, mesh=mesh, in_specs=(spec,), out_specs=spec, check_vma=False)
```

```python
import functools
import math

import jax
import jax.numpy as jnp
import ml_dtypes
import numpy as np
from jax import lax
from jax.experimental import pallas as pl
from jax.experimental.pallas import tpu as pltpu
from jax.sharding import PartitionSpec as P

TIME = 32
TAPERS = 12
FREQS = 2
COLS = 2 * TAPERS
ALL = FREQS * COLS
SUB = 8
HALF = 4
LANES = 128
PITCH = 56
LEAD = 8
CHUNKS = 4
BATCH = 4
MESH = pl.DeviceIdType.MESH
F32 = jnp.float32
BF16 = jnp.bfloat16


def taper_table():
    t = np.arange(TIME, dtype=np.float64)
    k = np.arange(TAPERS, dtype=np.float64)
    weights = math.sqrt(2.0 / (TIME + 1)) * np.sin(
        math.pi * (k[:, None] + 1.0) * (t[None, :] + 1.0) / (TIME + 1)
    )
    blocks = []
    for which in range(FREQS):
        phases = 2.0 * math.pi * (7 + 2 * which) * t / TIME
        pair = np.stack([weights * np.cos(phases), -weights * np.sin(phases)], axis=1)
        blocks.append(pair.reshape(COLS, TIME))
    return np.concatenate(blocks, axis=0).astype(np.float32).astype(ml_dtypes.bfloat16)


def lat_coefficients(grid_lon, grid_lat, bands):
    step_lon = 2.0 * math.pi / grid_lon
    step_lat = 2.6 / grid_lat
    cos_lat = np.cos(-1.3 + (np.arange(-1, grid_lat + 1) + 0.5) * step_lat)
    middle = cos_lat[1:-1]
    rows = np.stack(
        [
            1.0 / (2.0 * step_lon * middle),
            cos_lat[2:] / (2.0 * step_lat * middle),
            cos_lat[:-2] / (2.0 * step_lat * middle),
        ]
    ).astype(np.float32)
    rows = rows.reshape(3, bands, 1, LANES).transpose(1, 0, 2, 3)
    return np.broadcast_to(rows, (bands, 3, SUB, LANES)).copy()


def split(value, parts):
    pieces = []
    for _ in range(parts):
        piece = value.astype(BF16)
        pieces.append(piece)
        value = value - piece.astype(F32)
    return pieces


def iota(shape, dim):
    return lax.broadcasted_iota(jnp.int32, shape, dim)


def dot(a, b):
    return jnp.dot(a, b, preferred_element_type=F32)


def fields_kernel(
    n_lon, n_lat, levels, lon_cells, rows_total,
    winds, consts,
    x_out, mix_out,
    coef, tables, raw, padded, x_buf, pbuf, from_left, from_right, edges, row_first, row_last,
    row_prev, row_next, kept, gram, mine, lon_slots, band, lat_slots,
    in_sem, const_sem, out_sem, halo_send, halo_recv, lon_send, lon_recv, lat_send, lat_recv,
):
    lon = lax.axis_index("lon")
    lat = lax.axis_index("lat")
    groups = lon_cells // SUB
    blocks = 2 * TIME * levels
    per = 2 * TIME // CHUNKS
    cells = levels * lon_cells

    def load(c):
        part = pl.ds(c * per, per)
        return pltpu.make_async_copy(winds.at[part], raw.at[part], in_sem.at[c])

    for c in range(CHUNKS):
        load(c).start()
    band_rows = 3 * SUB
    get_coef = pltpu.make_async_copy(
        consts.at[pl.ds(pl.multiple_of(lat * band_rows, 8), band_rows)], coef, const_sem.at[0]
    )
    get_tables = pltpu.make_async_copy(
        consts.at[pl.ds(n_lat * band_rows, tables.shape[0])], tables, const_sem.at[1]
    )
    get_coef.start()
    get_tables.start()
    from_left[...] = jnp.zeros_like(from_left)
    from_right[...] = jnp.zeros_like(from_right)

    barrier = pltpu.get_barrier_semaphore()
    for d in range(1, n_lon):
        pl.semaphore_signal(
            barrier, inc=1, device_id=(lax.rem(lon + d, n_lon), lat), device_id_type=MESH
        )
    for d in range(1, n_lat):
        pl.semaphore_signal(
            barrier, inc=1, device_id=(lon, lax.rem(lat + d, n_lat)), device_id_type=MESH
        )

    pair = iota((SUB, LANES), 1) >> 1

    def widen(q, packed):
        x = raw[q].astype(F32)
        for l in range(levels):
            start = pl.multiple_of((q * levels + l) * PITCH + LEAD, 8)
            padded[pl.ds(start, lon_cells), :] = x[l * lon_cells:(l + 1) * lon_cells]
        turned = pltpu.roll(x, 2 * q + 1, 1).reshape(cells // SUB, SUB, LANES)
        return jnp.where((pair == q)[None], turned, packed)

    packed = jnp.zeros((cells // SUB, SUB, LANES), F32)
    for c in range(CHUNKS):
        load(c).wait()
        packed = lax.fori_loop(c * per, (c + 1) * per, widen, packed, unroll=16)
    pbuf[...] = packed.reshape(cells, LANES).astype(BF16)

    pl.semaphore_wait(barrier, n_lon + n_lat - 2)

    def remote(src, dst, send, recv, device):
        return pltpu.make_async_remote_copy(
            src_ref=src, dst_ref=dst, send_sem=send, recv_sem=recv,
            device_id=device, device_id_type=MESH,
        )

    up = remote(pbuf, from_left, halo_send.at[0], halo_recv.at[0], (lon, lax.rem(lat + 1, n_lat)))
    down = remote(
        pbuf, from_right, halo_send.at[1], halo_recv.at[1], (lon, lax.rem(lat + n_lat - 1, n_lat))
    )
    pl.when(lat < n_lat - 1)(lambda: up.start())
    pl.when(lat > 0)(lambda: down.start())

    row_first[...] = padded[pl.ds(LEAD, blocks, stride=PITCH), :].astype(BF16)
    row_last[...] = padded[pl.ds(LEAD + lon_cells - 1, blocks, stride=PITCH), :].astype(BF16)
    east = remote(
        row_last, row_prev, halo_send.at[2], halo_recv.at[2], (lax.rem(lon + 1, n_lon), lat)
    )
    west = remote(
        row_first, row_next, halo_send.at[3], halo_recv.at[3], (lax.rem(lon + n_lon - 1, n_lon), lat)
    )
    east.start()
    west.start()

    batch = BATCH
    lane = iota((batch * SUB, LANES), 1)
    first = lane == 0
    last = lane == LANES - 1
    get_coef.wait()
    along, ahead, behind = (
        jnp.concatenate([coef[i * SUB:(i + 1) * SUB, :]] * batch, axis=0) for i in range(3)
    )
    ahead_in = jnp.where(last, 0.0, ahead)
    behind_in = jnp.where(first, 0.0, behind)
    edge_factor = jnp.where(last, ahead, jnp.where(first, -behind, 0.0))

    low = (iota((SUB, LANES), 0) < HALF)[None]

    def add_gram(which):
        x = jnp.concatenate(
            [
                x_buf[:, column(slab + level, group, h)]
                for level, group in which for slab in (0, levels) for h in range(2)
            ],
            axis=1,
        )
        gram[...] += lax.dot_general(x, x, (((1,), (1,)), ((), ())), preferred_element_type=F32)

    def column(slab, group, h):
        pair = slab * (groups // 2) + group // 2
        at = (pair * 2 + h) * 2 + group % 2
        return pl.ds(at * LANES if isinstance(at, int) else pl.multiple_of(at * LANES, LANES), LANES)

    def without_halo(level, group, t0):
        base = pl.multiple_of(level * PITCH + group * SUB, SUB)
        d_lon, d_lat = [], []
        for comp in range(2):
            def rows(shift):
                parts = []
                for t in range(t0, t0 + batch):
                    offset = (comp * TIME + t) * levels * PITCH + LEAD + shift
                    parts.append(padded[pl.ds(base + offset, SUB), :])
                return jnp.concatenate(parts, axis=0)

            d_lon.append((rows(1) - rows(-1)) * along)
            center = rows(0)
            d_lat.append(
                pltpu.roll(center, LANES - 1, 1) * ahead_in - pltpu.roll(center, 1, 1) * behind_in
            )
        return d_lon[1] - d_lat[0], d_lon[0] + d_lat[1]

    def one_group(level, group, before, begun):
        add_gram([(level, before)])
        edge = edges[pl.ds(pl.multiple_of(level * lon_cells + group * SUB, SUB), SUB), :]
        for t0 in range(0, TIME, batch):
            halo = [
                edge_factor * jnp.concatenate(
                    [
                        pltpu.roll(edge, (LANES - 2 * (comp * TIME + t)) % LANES, 1)
                        for t in range(t0, t0 + batch)
                    ],
                    axis=0,
                )
                for comp in range(2)
            ]
            if begun:
                vort, div = (kept[f, t0 // batch, level, group] for f in range(2))
            else:
                vort, div = without_halo(level, group, t0)
            for slab, field in ((0, vort - halo[0]), (levels, div + halo[1])):
                by_t = field.reshape(batch // 2, 2, SUB, LANES)
                even, odd = by_t[:, 0], by_t[:, 1]
                crossed = pltpu.roll(jnp.where(low, odd, even), HALF, 1)
                halves = (jnp.where(low, even, crossed), jnp.where(low, crossed, odd))
                for h in range(2):
                    x_buf[pl.ds(t0 * HALF, batch * HALF), column(slab + level, group, h)] = (
                        halves[h].reshape(batch * HALF, LANES).astype(BF16)
                    )
    @pl.loop(0, levels)
    def _(level):
        def early(group, carry):
            for t0 in range(0, TIME, batch):
                vort, div = without_halo(level, group, t0)
                kept[0, t0 // batch, level, group] = vort
                kept[1, t0 // batch, level, group] = div
            return carry

        lax.fori_loop(1, groups - 1, early, 0, unroll=4)

    pl.when(lat > 0)(lambda: up.wait_recv())
    pl.when(lat < n_lat - 1)(lambda: down.wait_recv())
    edges[...] = jnp.where(
        iota((cells, LANES), 1) % 2 == 0,
        from_left[...].astype(F32),
        pltpu.roll(from_right[...].astype(F32), LANES - 2, 1),
    )
    gram[...] = jnp.zeros_like(gram)
    for slab in range(2 * levels):
        for h in range(2):
            x_buf[:, column(slab, 0, h)] = jnp.zeros((TIME * HALF, LANES), BF16)

    @pl.loop(0, levels)
    def _(level):
        def inner(group, carry):
            one_group(level, group, group - 1, True)
            return carry

        lax.fori_loop(1, groups - 1, inner, 0, unroll=4)

    east.wait_recv()
    padded[pl.ds(LEAD - 1, blocks, stride=PITCH), :] = row_prev[...].astype(F32)
    west.wait_recv()
    padded[pl.ds(LEAD + lon_cells, blocks, stride=PITCH), :] = row_next[...].astype(F32)

    @pl.loop(0, levels)
    def _(level):
        def outer(end, carry):
            one_group(level, end * (groups - 1), (1 - end) * (groups - 2), False)
            return carry

        lax.fori_loop(0, 2, outer, 0, unroll=2)

    add_gram([(level, groups - 1) for level in range(levels)])
    store = pltpu.make_async_copy(x_buf, x_out, out_sem)
    store.start()

    side = TIME * HALF
    same = iota((side, side), 0) % HALF == iota((side, side), 1) % HALF
    fold = (iota((side, LANES), 0) // HALF == iota((side, LANES), 1)).astype(F32).astype(BF16)
    fold_t = (iota((TIME, side), 0) == iota((TIME, side), 1) // HALF).astype(F32).astype(BF16)
    masked = jnp.where(same, gram[...], 0.0)
    by_time = dot(
        jnp.concatenate([fold_t] * 3, axis=1), jnp.concatenate(split(masked, 3), axis=0)
    )
    folded = dot(jnp.concatenate(split(by_time, 3), axis=0), fold)
    times = folded[:TIME] + folded[TIME:2 * TIME] + folded[2 * TIME:]
    tile = times[:SUB]
    for a in range(1, TIME // SUB):
        tile = tile + pltpu.roll(times[a * SUB:(a + 1) * SUB], a * TIME, 1)
    mine[...] = tile

    lon_copies = [
        remote(mine, lon_slots.at[d - 1], lon_send.at[d - 1], lon_recv.at[d - 1],
               (lax.rem(lon + d, n_lon), lat))
        for d in range(1, n_lon)
    ]
    for copy in lon_copies:
        copy.start()
    get_tables.wait()
    table3 = tables[:ALL, :].astype(BF16)
    table_aug = tables[ALL:2 * ALL, :]
    table_t = tables[2 * ALL:, :].astype(BF16)
    spread = (iota((LANES, side), 0) - 64 == iota((LANES, side), 1) // HALF).astype(F32).astype(BF16)
    tall = ALL * HALF
    r = iota((2 * tall, ALL), 0)
    source = jnp.where(r < tall, r >> 2, ((r - tall) >> 2) ^ 1)
    pick = (source == iota((2 * tall, ALL), 1)).astype(F32).astype(BF16)
    total = mine[...]
    for d, copy in enumerate(lon_copies):
        copy.wait_recv()
        total = total + lon_slots[d]
    band[...] = total
    lat_copies = [
        remote(band, lat_slots.at[d - 1], lat_send.at[d - 1], lat_recv.at[d - 1],
               (lon, lax.rem(lat + d, n_lat)))
        for d in range(1, n_lat)
    ]
    for copy in lat_copies:
        copy.start()
    total = band[...]
    for d, copy in enumerate(lat_copies):
        copy.wait_recv()
        total = total + lat_slots[d]

    total = total * (1.0 / rows_total)
    square = jnp.concatenate(
        [total] + [pltpu.roll(total, LANES - a * TIME, 1) for a in range(1, TIME // SUB)], axis=0
    )
    stacked = split(square, 3) + [jnp.zeros((TIME, LANES), BF16)]
    half = dot(table3, jnp.concatenate(stacked, axis=0))
    full = dot(jnp.concatenate(split(half, 3), axis=0), table_t)
    full = full[:ALL] + full[ALL:2 * ALL] + full[2 * ALL:]
    aug = jnp.where(iota((ALL, LANES), 1) < 64, full, table_aug)
    row = iota((COLS, LANES), 0)
    lane_a = iota((COLS, LANES), 1)
    parts = [aug[:COLS], aug[COLS:]]
    panel = 8
    for start in range(0, COLS, panel):
        columns = [
            [
                jnp.broadcast_to(parts[f][:, at:at + 1], (COLS, LANES))
                for at in range(f * COLS + start, f * COLS + start + panel)
            ]
            for f in range(FREQS)
        ]
        for j in range(panel):
            k = start + j
            for f in range(FREQS):
                cols = columns[f]
                pivot = cols[j][k:k + 1, :]
                guess = pl.reciprocal(pivot, approx=True)
                inverse = guess * (2.0 - pivot * guess)
                scale = jnp.where(row > k, cols[j] * inverse, 0.0)
                for i in range(j + 1, panel):
                    cols[i] = cols[i] - scale * cols[i][k:k + 1, :]
                parts[f] = parts[f] - scale * parts[f][k:k + 1, :]
    rows_done = []
    for f in range(FREQS):
        on_diag = lane_a == iota((COLS, LANES), 0) + f * COLS
        diag = jnp.sum(jnp.where(on_diag, parts[f], 0.0), axis=1, keepdims=True)
        rows_done.append(parts[f] / jnp.sqrt(diag))
    mix = jnp.concatenate(rows_done, axis=0)
    parts = dot(jnp.concatenate(split(mix, 2), axis=0), spread).astype(BF16)
    wide_mix = jnp.concatenate([parts[:ALL], parts[ALL:]], axis=1)
    spread_rows = dot(pick, wide_mix)
    keep = (iota((2 * tall, 2 * side), 0) & 3) == (iota((2 * tall, 2 * side), 1) & 3)
    mix_out[...] = jnp.where(keep, spread_rows, 0.0).astype(BF16)

    pl.when(lat < n_lat - 1)(lambda: up.wait_send())
    pl.when(lat > 0)(lambda: down.wait_send())
    for copy in [east, west] + lon_copies + lat_copies:
        copy.wait_send()
    store.wait()


def basis_kernel(mix_buf, x_buf, out, out_buf, out_sem):
    slabs, lon_cells = out.shape[2], out.shape[3]
    width = lon_cells // HALF * LANES
    pairs = lon_cells // (2 * SUB)
    tall = ALL * HALF
    low = (iota((SUB, LANES), 0) < HALF)[None]

    def put(i, g):
        part = (slice(None), slice(None), i, pl.ds(g * 2 * SUB, 2 * SUB))
        return pltpu.make_async_copy(out_buf.at[part], out.at[part], out_sem.at[i, g])

    @pl.loop(0, slabs, unroll=4)
    def _(i):
        for g in range(pairs):
            res = []
            for h in range(2):
                at = pl.multiple_of(i * width + (2 * g + h) * 2 * LANES, LANES)
                part = x_buf[:, pl.ds(at, 2 * LANES)]
                rows = mix_buf[h * tall:(h + 1) * tall, :]
                res.append(dot(rows, jnp.concatenate([part, part], axis=0)))
            for w in range(2):
                near, far = (
                    r[:, w * LANES:(w + 1) * LANES].reshape(ALL // 2, SUB, LANES) for r in res
                )
                here = slice((2 * g + w) * SUB, (2 * g + w + 1) * SUB)
                out_buf[:, 0, i, here, :] = jnp.where(low, near, far)
                out_buf[:, 1, i, here, :] = pltpu.roll(jnp.where(low, far, near), HALF, 1)
            put(i, g).start()

    @pl.loop(0, slabs)
    def _(i):
        for g in range(pairs):
            put(i, g).wait()


def body(n_lon, n_lat, winds):
    _, times, levels, lon_cells, lat_cells = winds.shape
    cells = levels * lon_cells
    columns = 2 * cells // HALF * LANES
    side = TIME * HALF
    table = taper_table().astype(np.float32)
    used = n_lat * 3 * SUB + 2 * ALL + LANES
    consts = np.zeros((8192, LANES), np.float32)
    coef = lat_coefficients(n_lon * lon_cells, n_lat * lat_cells, n_lat)
    consts[:n_lat * 3 * SUB] = coef.reshape(-1, LANES)
    tables = consts[n_lat * 3 * SUB:used]
    tables[:ALL, :3 * TIME] = np.concatenate([table] * 3, axis=1)
    tables[ALL:2 * ALL, 64:64 + TIME] = table
    tables[2 * ALL:2 * ALL + TIME, :ALL] = table.T
    rows_total = 2 * levels * lon_cells * n_lon * lat_cells * n_lat
    vmem = pl.BlockSpec(memory_space=pltpu.VMEM)
    anywhere = pl.BlockSpec(memory_space=pl.ANY)
    hbm = pl.BlockSpec(memory_space=pltpu.HBM)
    blocks = 2 * TIME * levels
    dma = pltpu.SemaphoreType.DMA
    x, mix = pl.pallas_call(
        functools.partial(fields_kernel, n_lon, n_lat, levels, lon_cells, rows_total),
        out_shape=(
            jax.ShapeDtypeStruct((side, columns), BF16),
            jax.ShapeDtypeStruct((2 * ALL * HALF, 2 * side), BF16),
        ),
        in_specs=[hbm, hbm],
        out_specs=(anywhere, vmem),
        scratch_shapes=[
            pltpu.VMEM((3 * SUB, LANES), F32),
            pltpu.VMEM((2 * ALL + LANES, LANES), F32),
            pltpu.VMEM((2 * TIME, cells, LANES), BF16),
            pltpu.VMEM(((blocks + 1) * PITCH + LEAD, LANES), F32),
            pltpu.VMEM((side, columns), BF16),
            pltpu.VMEM((cells, LANES), BF16),
            pltpu.VMEM((cells, LANES), BF16),
            pltpu.VMEM((cells, LANES), BF16),
            pltpu.VMEM((cells, LANES), F32),
            pltpu.VMEM((blocks, LANES), BF16),
            pltpu.VMEM((blocks, LANES), BF16),
            pltpu.VMEM((blocks, LANES), BF16),
            pltpu.VMEM((blocks, LANES), BF16),
            pltpu.VMEM((2, TIME // BATCH, levels, lon_cells // SUB, BATCH * SUB, LANES), F32),
            pltpu.VMEM((side, side), F32),
            pltpu.VMEM((SUB, LANES), F32),
            pltpu.VMEM((n_lon - 1, SUB, LANES), F32),
            pltpu.VMEM((SUB, LANES), F32),
            pltpu.VMEM((n_lat - 1, SUB, LANES), F32),
            dma((CHUNKS,)),
            dma((2,)),
            dma(()),
            dma((4,)),
            dma((4,)),
            dma((n_lon - 1,)),
            dma((n_lon - 1,)),
            dma((n_lat - 1,)),
            dma((n_lat - 1,)),
        ],
        compiler_params=pltpu.CompilerParams(
            collective_id=0, has_side_effects=True, vmem_limit_bytes=50 * 2**20
        ),
        name="fields",
    )(
        winds.reshape(2 * TIME, cells, LANES),
        jnp.asarray(consts),
    )
    basis = pl.pallas_call(
        basis_kernel,
        out_shape=jax.ShapeDtypeStruct((ALL // 2, 2, 2 * levels, lon_cells, LANES), F32),
        in_specs=[vmem, vmem],
        out_specs=hbm,
        scratch_shapes=[
            pltpu.VMEM((ALL // 2, 2, 2 * levels, lon_cells, LANES), F32),
            dma((2 * levels, lon_cells // (2 * SUB))),
        ],
        compiler_params=pltpu.CompilerParams(vmem_limit_bytes=20 * 2**20),
        name="basis",
    )(mix, x)
    return basis.reshape(ALL, 2, levels, lon_cells, lat_cells)


def solution(mesh):
    spec = P(None, None, None, "lon", "lat")
    run = functools.partial(body, mesh.shape["lon"], mesh.shape["lat"])
    return jax.shard_map(run, mesh=mesh, in_specs=(spec,), out_specs=spec, check_vma=False)
```

```python
import functools
import math

import jax
import jax.numpy as jnp
import ml_dtypes
import numpy as np
from jax import lax
from jax.experimental import pallas as pl
from jax.experimental.pallas import tpu as pltpu
from jax.sharding import PartitionSpec as P

TIME = 32
TAPERS = 12
FREQS = 2
COLS = 2 * TAPERS
ALL = FREQS * COLS
SUB = 8
HALF = 4
LANES = 128
PITCH = 56
LEAD = 8
CHUNKS = 4
BATCH = 4
MESH = pl.DeviceIdType.MESH
F32 = jnp.float32
BF16 = jnp.bfloat16


def taper_table():
    t = np.arange(TIME, dtype=np.float64)
    k = np.arange(TAPERS, dtype=np.float64)
    weights = math.sqrt(2.0 / (TIME + 1)) * np.sin(
        math.pi * (k[:, None] + 1.0) * (t[None, :] + 1.0) / (TIME + 1)
    )
    blocks = []
    for which in range(FREQS):
        phases = 2.0 * math.pi * (7 + 2 * which) * t / TIME
        pair = np.stack([weights * np.cos(phases), -weights * np.sin(phases)], axis=1)
        blocks.append(pair.reshape(COLS, TIME))
    return np.concatenate(blocks, axis=0).astype(np.float32).astype(ml_dtypes.bfloat16)


def lat_coefficients(grid_lon, grid_lat, bands):
    step_lon = 2.0 * math.pi / grid_lon
    step_lat = 2.6 / grid_lat
    cos_lat = np.cos(-1.3 + (np.arange(-1, grid_lat + 1) + 0.5) * step_lat)
    middle = cos_lat[1:-1]
    rows = np.stack(
        [
            1.0 / (2.0 * step_lon * middle),
            cos_lat[2:] / (2.0 * step_lat * middle),
            cos_lat[:-2] / (2.0 * step_lat * middle),
        ]
    ).astype(np.float32)
    rows = rows.reshape(3, bands, 1, LANES).transpose(1, 0, 2, 3)
    return np.broadcast_to(rows, (bands, 3, SUB, LANES)).copy()


def split(value, parts):
    pieces = []
    for _ in range(parts):
        piece = value.astype(BF16)
        pieces.append(piece)
        value = value - piece.astype(F32)
    return pieces


def iota(shape, dim):
    return lax.broadcasted_iota(jnp.int32, shape, dim)


def dot(a, b):
    return jnp.dot(a, b, preferred_element_type=F32)


def fields_kernel(
    n_lon, n_lat, levels, lon_cells, rows_total,
    winds, consts,
    x_out, mix_out,
    coef, tables, raw, padded, x_buf, pbuf, from_left, from_right, edges, row_first, row_last,
    row_prev, row_next, kept, gram, mine, lon_slots, band, lat_slots,
    in_sem, const_sem, out_sem, halo_send, halo_recv, lon_send, lon_recv, lat_send, lat_recv,
):
    lon = lax.axis_index("lon")
    lat = lax.axis_index("lat")
    groups = lon_cells // SUB
    blocks = 2 * TIME * levels
    per = 2 * TIME // CHUNKS
    cells = levels * lon_cells

    def load(c):
        part = pl.ds(c * per, per)
        return pltpu.make_async_copy(winds.at[part], raw.at[part], in_sem.at[c])

    for c in range(CHUNKS):
        load(c).start()
    band_rows = 3 * SUB
    get_coef = pltpu.make_async_copy(
        consts.at[pl.ds(pl.multiple_of(lat * band_rows, 8), band_rows)], coef, const_sem.at[0]
    )
    get_tables = pltpu.make_async_copy(
        consts.at[pl.ds(n_lat * band_rows, tables.shape[0])], tables, const_sem.at[1]
    )
    get_coef.start()
    get_tables.start()
    from_left[...] = jnp.zeros_like(from_left)
    from_right[...] = jnp.zeros_like(from_right)

    barrier = pltpu.get_barrier_semaphore()
    for d in range(1, n_lon):
        pl.semaphore_signal(
            barrier, inc=1, device_id=(lax.rem(lon + d, n_lon), lat), device_id_type=MESH
        )
    for d in range(1, n_lat):
        pl.semaphore_signal(
            barrier, inc=1, device_id=(lon, lax.rem(lat + d, n_lat)), device_id_type=MESH
        )

    pair = iota((SUB, LANES), 1) >> 1

    def widen(q, packed):
        x = raw[q].astype(F32)
        for l in range(levels):
            start = pl.multiple_of((q * levels + l) * PITCH + LEAD, 8)
            padded[pl.ds(start, lon_cells), :] = x[l * lon_cells:(l + 1) * lon_cells]
        turned = pltpu.roll(x, 2 * q + 1, 1).reshape(cells // SUB, SUB, LANES)
        return jnp.where((pair == q)[None], turned, packed)

    packed = jnp.zeros((cells // SUB, SUB, LANES), F32)
    for c in range(CHUNKS):
        load(c).wait()
        packed = lax.fori_loop(c * per, (c + 1) * per, widen, packed, unroll=16)
    pbuf[...] = packed.reshape(cells, LANES).astype(BF16)

    pl.semaphore_wait(barrier, n_lon + n_lat - 2)

    def remote(src, dst, send, recv, device):
        return pltpu.make_async_remote_copy(
            src_ref=src, dst_ref=dst, send_sem=send, recv_sem=recv,
            device_id=device, device_id_type=MESH,
        )

    up = remote(pbuf, from_left, halo_send.at[0], halo_recv.at[0], (lon, lax.rem(lat + 1, n_lat)))
    down = remote(
        pbuf, from_right, halo_send.at[1], halo_recv.at[1], (lon, lax.rem(lat + n_lat - 1, n_lat))
    )
    pl.when(lat < n_lat - 1)(lambda: up.start())
    pl.when(lat > 0)(lambda: down.start())

    row_first[...] = padded[pl.ds(LEAD, blocks, stride=PITCH), :].astype(BF16)
    row_last[...] = padded[pl.ds(LEAD + lon_cells - 1, blocks, stride=PITCH), :].astype(BF16)
    east = remote(
        row_last, row_prev, halo_send.at[2], halo_recv.at[2], (lax.rem(lon + 1, n_lon), lat)
    )
    west = remote(
        row_first, row_next, halo_send.at[3], halo_recv.at[3], (lax.rem(lon + n_lon - 1, n_lon), lat)
    )
    east.start()
    west.start()

    batch = BATCH
    lane = iota((batch * SUB, LANES), 1)
    first = lane == 0
    last = lane == LANES - 1
    get_coef.wait()
    along, ahead, behind = (
        jnp.concatenate([coef[i * SUB:(i + 1) * SUB, :]] * batch, axis=0) for i in range(3)
    )
    ahead_in = jnp.where(last, 0.0, ahead)
    behind_in = jnp.where(first, 0.0, behind)
    edge_factor = jnp.where(last, ahead, jnp.where(first, -behind, 0.0))

    low = (iota((SUB, LANES), 0) < HALF)[None]

    def add_gram(which):
        x = jnp.concatenate(
            [
                x_buf[:, column(slab + level, group, h)]
                for level, group in which for slab in (0, levels) for h in range(2)
            ],
            axis=1,
        )
        gram[...] += lax.dot_general(x, x, (((1,), (1,)), ((), ())), preferred_element_type=F32)

    def column(slab, group, h):
        pair = slab * (groups // 2) + group // 2
        at = (pair * 2 + h) * 2 + group % 2
        return pl.ds(at * LANES if isinstance(at, int) else pl.multiple_of(at * LANES, LANES), LANES)

    def without_halo(level, group, t0):
        base = pl.multiple_of(level * PITCH + group * SUB, SUB)
        d_lon, d_lat = [], []
        for comp in range(2):
            def rows(shift):
                parts = []
                for t in range(t0, t0 + batch):
                    offset = (comp * TIME + t) * levels * PITCH + LEAD + shift
                    parts.append(padded[pl.ds(base + offset, SUB), :])
                return jnp.concatenate(parts, axis=0)

            d_lon.append((rows(1) - rows(-1)) * along)
            center = rows(0)
            d_lat.append(
                pltpu.roll(center, LANES - 1, 1) * ahead_in - pltpu.roll(center, 1, 1) * behind_in
            )
        return d_lon[1] - d_lat[0], d_lon[0] + d_lat[1]

    def one_group(level, group, before, begun):
        add_gram([(level, before)])
        edge = edges[pl.ds(pl.multiple_of(level * lon_cells + group * SUB, SUB), SUB), :]
        for t0 in range(0, TIME, batch):
            halo = [
                edge_factor * jnp.concatenate(
                    [
                        pltpu.roll(edge, (LANES - 2 * (comp * TIME + t)) % LANES, 1)
                        for t in range(t0, t0 + batch)
                    ],
                    axis=0,
                )
                for comp in range(2)
            ]
            if begun:
                vort, div = (kept[f, t0 // batch, level, group] for f in range(2))
            else:
                vort, div = without_halo(level, group, t0)
            for slab, field in ((0, vort - halo[0]), (levels, div + halo[1])):
                by_t = field.reshape(batch // 2, 2, SUB, LANES)
                even, odd = by_t[:, 0], by_t[:, 1]
                crossed = pltpu.roll(jnp.where(low, odd, even), HALF, 1)
                halves = (jnp.where(low, even, crossed), jnp.where(low, crossed, odd))
                for h in range(2):
                    x_buf[pl.ds(t0 * HALF, batch * HALF), column(slab + level, group, h)] = (
                        halves[h].reshape(batch * HALF, LANES).astype(BF16)
                    )
    @pl.loop(0, levels, unroll=2)
    def _(level):
        def early(group, carry):
            for t0 in range(0, TIME, batch):
                vort, div = without_halo(level, group, t0)
                kept[0, t0 // batch, level, group] = vort
                kept[1, t0 // batch, level, group] = div
            return carry

        lax.fori_loop(1, groups - 1, early, 0, unroll=4)

    pl.when(lat > 0)(lambda: up.wait_recv())
    pl.when(lat < n_lat - 1)(lambda: down.wait_recv())
    edges[...] = jnp.where(
        iota((cells, LANES), 1) % 2 == 0,
        from_left[...].astype(F32),
        pltpu.roll(from_right[...].astype(F32), LANES - 2, 1),
    )
    gram[...] = jnp.zeros_like(gram)
    for slab in range(2 * levels):
        for h in range(2):
            x_buf[:, column(slab, 0, h)] = jnp.zeros((TIME * HALF, LANES), BF16)

    @pl.loop(0, levels, unroll=2)
    def _(level):
        def inner(group, carry):
            one_group(level, group, group - 1, True)
            return carry

        lax.fori_loop(1, groups - 1, inner, 0, unroll=4)

    east.wait_recv()
    padded[pl.ds(LEAD - 1, blocks, stride=PITCH), :] = row_prev[...].astype(F32)
    west.wait_recv()
    padded[pl.ds(LEAD + lon_cells, blocks, stride=PITCH), :] = row_next[...].astype(F32)

    @pl.loop(0, levels, unroll=2)
    def _(level):
        def outer(end, carry):
            one_group(level, end * (groups - 1), (1 - end) * (groups - 2), False)
            return carry

        lax.fori_loop(0, 2, outer, 0, unroll=2)

    add_gram([(level, groups - 1) for level in range(levels)])
    store = pltpu.make_async_copy(x_buf, x_out, out_sem)
    store.start()

    side = TIME * HALF
    same = iota((side, side), 0) % HALF == iota((side, side), 1) % HALF
    fold = (iota((side, LANES), 0) // HALF == iota((side, LANES), 1)).astype(F32).astype(BF16)
    fold_t = (iota((TIME, side), 0) == iota((TIME, side), 1) // HALF).astype(F32).astype(BF16)
    masked = jnp.where(same, gram[...], 0.0)
    by_time = dot(
        jnp.concatenate([fold_t] * 3, axis=1), jnp.concatenate(split(masked, 3), axis=0)
    )
    folded = dot(jnp.concatenate(split(by_time, 3), axis=0), fold)
    times = folded[:TIME] + folded[TIME:2 * TIME] + folded[2 * TIME:]
    tile = times[:SUB]
    for a in range(1, TIME // SUB):
        tile = tile + pltpu.roll(times[a * SUB:(a + 1) * SUB], a * TIME, 1)
    mine[...] = tile

    lon_copies = [
        remote(mine, lon_slots.at[d - 1], lon_send.at[d - 1], lon_recv.at[d - 1],
               (lax.rem(lon + d, n_lon), lat))
        for d in range(1, n_lon)
    ]
    for copy in lon_copies:
        copy.start()
    get_tables.wait()
    table3 = tables[:ALL, :].astype(BF16)
    table_aug = tables[ALL:2 * ALL, :]
    table_t = tables[2 * ALL:, :].astype(BF16)
    spread = (iota((LANES, side), 0) - 64 == iota((LANES, side), 1) // HALF).astype(F32).astype(BF16)
    tall = ALL * HALF
    r = iota((2 * tall, ALL), 0)
    source = jnp.where(r < tall, r >> 2, ((r - tall) >> 2) ^ 1)
    pick = (source == iota((2 * tall, ALL), 1)).astype(F32).astype(BF16)
    total = mine[...]
    for d, copy in enumerate(lon_copies):
        copy.wait_recv()
        total = total + lon_slots[d]
    band[...] = total
    lat_copies = [
        remote(band, lat_slots.at[d - 1], lat_send.at[d - 1], lat_recv.at[d - 1],
               (lon, lax.rem(lat + d, n_lat)))
        for d in range(1, n_lat)
    ]
    for copy in lat_copies:
        copy.start()
    total = band[...]
    for d, copy in enumerate(lat_copies):
        copy.wait_recv()
        total = total + lat_slots[d]

    total = total * (1.0 / rows_total)
    square = jnp.concatenate(
        [total] + [pltpu.roll(total, LANES - a * TIME, 1) for a in range(1, TIME // SUB)], axis=0
    )
    stacked = split(square, 3) + [jnp.zeros((TIME, LANES), BF16)]
    half = dot(table3, jnp.concatenate(stacked, axis=0))
    full = dot(jnp.concatenate(split(half, 3), axis=0), table_t)
    full = full[:ALL] + full[ALL:2 * ALL] + full[2 * ALL:]
    aug = jnp.where(iota((ALL, LANES), 1) < 64, full, table_aug)
    row = iota((COLS, LANES), 0)
    lane_a = iota((COLS, LANES), 1)
    parts = [aug[:COLS], aug[COLS:]]
    panel = 8
    for start in range(0, COLS, panel):
        columns = [
            [
                jnp.broadcast_to(parts[f][:, at:at + 1], (COLS, LANES))
                for at in range(f * COLS + start, f * COLS + start + panel)
            ]
            for f in range(FREQS)
        ]
        for j in range(panel):
            k = start + j
            for f in range(FREQS):
                cols = columns[f]
                pivot = cols[j][k:k + 1, :]
                guess = pl.reciprocal(pivot, approx=True)
                inverse = guess * (2.0 - pivot * guess)
                scale = jnp.where(row > k, cols[j] * inverse, 0.0)
                for i in range(j + 1, panel):
                    cols[i] = cols[i] - scale * cols[i][k:k + 1, :]
                parts[f] = parts[f] - scale * parts[f][k:k + 1, :]
    rows_done = []
    for f in range(FREQS):
        on_diag = lane_a == iota((COLS, LANES), 0) + f * COLS
        diag = jnp.sum(jnp.where(on_diag, parts[f], 0.0), axis=1, keepdims=True)
        rows_done.append(parts[f] / jnp.sqrt(diag))
    mix = jnp.concatenate(rows_done, axis=0)
    parts = dot(jnp.concatenate(split(mix, 2), axis=0), spread).astype(BF16)
    wide_mix = jnp.concatenate([parts[:ALL], parts[ALL:]], axis=1)
    spread_rows = dot(pick, wide_mix)
    keep = (iota((2 * tall, 2 * side), 0) & 3) == (iota((2 * tall, 2 * side), 1) & 3)
    mix_out[...] = jnp.where(keep, spread_rows, 0.0).astype(BF16)

    pl.when(lat < n_lat - 1)(lambda: up.wait_send())
    pl.when(lat > 0)(lambda: down.wait_send())
    for copy in [east, west] + lon_copies + lat_copies:
        copy.wait_send()
    store.wait()


def basis_kernel(mix_buf, x_buf, out, out_buf, out_sem):
    slabs, lon_cells = out.shape[2], out.shape[3]
    width = lon_cells // HALF * LANES
    pairs = lon_cells // (2 * SUB)
    tall = ALL * HALF
    low = (iota((SUB, LANES), 0) < HALF)[None]

    def put(i, g):
        part = (slice(None), slice(None), i, pl.ds(g * 2 * SUB, 2 * SUB))
        return pltpu.make_async_copy(out_buf.at[part], out.at[part], out_sem.at[i, g])

    @pl.loop(0, slabs, unroll=4)
    def _(i):
        for g in range(pairs):
            res = []
            for h in range(2):
                at = pl.multiple_of(i * width + (2 * g + h) * 2 * LANES, LANES)
                part = x_buf[:, pl.ds(at, 2 * LANES)]
                rows = mix_buf[h * tall:(h + 1) * tall, :]
                res.append(dot(rows, jnp.concatenate([part, part], axis=0)))
            for w in range(2):
                near, far = (
                    r[:, w * LANES:(w + 1) * LANES].reshape(ALL // 2, SUB, LANES) for r in res
                )
                here = slice((2 * g + w) * SUB, (2 * g + w + 1) * SUB)
                out_buf[:, 0, i, here, :] = jnp.where(low, near, far)
                out_buf[:, 1, i, here, :] = pltpu.roll(jnp.where(low, far, near), HALF, 1)
            put(i, g).start()

    @pl.loop(0, slabs)
    def _(i):
        for g in range(pairs):
            put(i, g).wait()


def body(n_lon, n_lat, winds):
    _, times, levels, lon_cells, lat_cells = winds.shape
    cells = levels * lon_cells
    columns = 2 * cells // HALF * LANES
    side = TIME * HALF
    table = taper_table().astype(np.float32)
    used = n_lat * 3 * SUB + 2 * ALL + LANES
    consts = np.zeros((8192, LANES), np.float32)
    coef = lat_coefficients(n_lon * lon_cells, n_lat * lat_cells, n_lat)
    consts[:n_lat * 3 * SUB] = coef.reshape(-1, LANES)
    tables = consts[n_lat * 3 * SUB:used]
    tables[:ALL, :3 * TIME] = np.concatenate([table] * 3, axis=1)
    tables[ALL:2 * ALL, 64:64 + TIME] = table
    tables[2 * ALL:2 * ALL + TIME, :ALL] = table.T
    rows_total = 2 * levels * lon_cells * n_lon * lat_cells * n_lat
    vmem = pl.BlockSpec(memory_space=pltpu.VMEM)
    anywhere = pl.BlockSpec(memory_space=pl.ANY)
    hbm = pl.BlockSpec(memory_space=pltpu.HBM)
    blocks = 2 * TIME * levels
    dma = pltpu.SemaphoreType.DMA
    x, mix = pl.pallas_call(
        functools.partial(fields_kernel, n_lon, n_lat, levels, lon_cells, rows_total),
        out_shape=(
            jax.ShapeDtypeStruct((side, columns), BF16),
            jax.ShapeDtypeStruct((2 * ALL * HALF, 2 * side), BF16),
        ),
        in_specs=[hbm, hbm],
        out_specs=(anywhere, vmem),
        scratch_shapes=[
            pltpu.VMEM((3 * SUB, LANES), F32),
            pltpu.VMEM((2 * ALL + LANES, LANES), F32),
            pltpu.VMEM((2 * TIME, cells, LANES), BF16),
            pltpu.VMEM(((blocks + 1) * PITCH + LEAD, LANES), F32),
            pltpu.VMEM((side, columns), BF16),
            pltpu.VMEM((cells, LANES), BF16),
            pltpu.VMEM((cells, LANES), BF16),
            pltpu.VMEM((cells, LANES), BF16),
            pltpu.VMEM((cells, LANES), F32),
            pltpu.VMEM((blocks, LANES), BF16),
            pltpu.VMEM((blocks, LANES), BF16),
            pltpu.VMEM((blocks, LANES), BF16),
            pltpu.VMEM((blocks, LANES), BF16),
            pltpu.VMEM((2, TIME // BATCH, levels, lon_cells // SUB, BATCH * SUB, LANES), F32),
            pltpu.VMEM((side, side), F32),
            pltpu.VMEM((SUB, LANES), F32),
            pltpu.VMEM((n_lon - 1, SUB, LANES), F32),
            pltpu.VMEM((SUB, LANES), F32),
            pltpu.VMEM((n_lat - 1, SUB, LANES), F32),
            dma((CHUNKS,)),
            dma((2,)),
            dma(()),
            dma((4,)),
            dma((4,)),
            dma((n_lon - 1,)),
            dma((n_lon - 1,)),
            dma((n_lat - 1,)),
            dma((n_lat - 1,)),
        ],
        compiler_params=pltpu.CompilerParams(
            collective_id=0, has_side_effects=True, vmem_limit_bytes=50 * 2**20
        ),
        name="fields",
    )(
        winds.reshape(2 * TIME, cells, LANES),
        jnp.asarray(consts),
    )
    basis = pl.pallas_call(
        basis_kernel,
        out_shape=jax.ShapeDtypeStruct((ALL // 2, 2, 2 * levels, lon_cells, LANES), F32),
        in_specs=[vmem, vmem],
        out_specs=hbm,
        scratch_shapes=[
            pltpu.VMEM((ALL // 2, 2, 2 * levels, lon_cells, LANES), F32),
            dma((2 * levels, lon_cells // (2 * SUB))),
        ],
        compiler_params=pltpu.CompilerParams(vmem_limit_bytes=20 * 2**20),
        name="basis",
    )(mix, x)
    return basis.reshape(ALL, 2, levels, lon_cells, lat_cells)


def solution(mesh):
    spec = P(None, None, None, "lon", "lat")
    run = functools.partial(body, mesh.shape["lon"], mesh.shape["lat"])
    return jax.shard_map(run, mesh=mesh, in_specs=(spec,), out_specs=spec, check_vma=False)
```
